1024 devices in a mesh: dp: 8 (over y), ctx: 4 (over x_lo, core), tp: 32 (over z, x_hi).
Axes of the slice: x: 8 (x_hi: 4, x_lo: 2; x = x_hi * 2 + x_lo), y: 8, z: 8, core: 2. Of those that a mesh axis runs over, the one named last changes fastest.
Arguments:
- tokens: bfloat16 [4, 64, 4096], P('ctx', 'dp'), may hold values from -6 to 6
- cotangent: bfloat16 [4, 64, 4096], P('ctx', 'dp'), may hold values from -6 to 6
- routes: int32 [4, 64, 8], P('ctx'), may hold values from 0 to 127, all different within a row; in each aligned block of 64 rows (0 to 63, 64 to 127, ..., all dimensions but the last counted through in order) at most 6 rows name the same one
- probs: bfloat16 [4, 64, 8], P('ctx'), may hold values from 0.029907227 to 0.3984375
- w_gate: bfloat16 [128, 4096, 1024], P(('ctx', 'tp'), None, 'dp'), may hold values from -0.09375 to 0.09375
- w_up: bfloat16 [128, 4096, 1024], P(('ctx', 'tp'), None, 'dp'), may hold values from -0.09375 to 0.09375
- w_down: bfloat16 [128, 1024, 4096], P(('ctx', 'tp'), 'dp'), may hold values from -0.1875 to 0.1875
Outputs:
- mixed: bfloat16 [4, 64, 4096], P('ctx', 'tp', 'dp')
- input_grad: bfloat16 [4, 64, 4096], P('ctx', 'tp', 'dp')
The draws below stay inside these ranges and needn't reach their ends.
Inputs may be any that keep to these rules, and one draw needn't show every extreme that they name: `routes`: in each column every expert is named by at most 6 of its 64 rows, and a token never names one expert twice.
All inputs are finite; a program needn't handle non-finite values.
Results may differ from the reference program's by a relative error of at most 0.023.
Values may be sent and summed in bfloat16 or wider, within the bound.
No kernel may reach another device: no remote copies, remote signals or barrier semaphores. Data moves between devices by JAX's collectives and lax.ppermute only.
A program may use at most 32 MiB of HBM per device.

```python
import math
import jax
import jax.numpy as jnp
import numpy as np
from jax import lax

D = 4096
FF = 1024
TOP = 8
NCOL = 4
COLUMN = 64
EXPERTS = 128
CAP = 6
N_DP = 8


def levels(key, shape, shards, least, largest):
    factor_of = 1.0
    for axis_at, parts in shards:
        heights = jax.random.uniform(jax.random.fold_in(jax.random.fold_in(key, 6), axis_at), (parts,), jnp.float32, least / len(shards), largest / len(shards))
        factor_of = factor_of * jnp.repeat(jnp.exp(heights), shape[axis_at] // parts).reshape((-1,) + (1,) * (len(shape) - 1 - axis_at))
    return factor_of


def routed_block(key, own, number, rows, amount, top, limit, skew):
    order = jax.random.permutation(key, amount)
    crowded, usual = portions_of(amount, rows * top, limit, skew, True), portions_of(amount, rows * top, limit, skew, False)
    places = jnp.arange(amount)

    def named(sizes, turn):
        used = int((sizes > 0).sum())
        fixed = max(1, used // 4)
        shifted = fixed + (places - fixed + turn * (used - fixed)) % max(1, amount - fixed)
        return jnp.zeros((amount,), jnp.int32).at[order[jnp.where(places < fixed, places, shifted)]].set(jnp.asarray(sizes, jnp.int32))

    sizes = jnp.where(number % 4 == 0, named(crowded, number // 4), named(usual, number - number // 4 - 1))
    mixed = jax.random.permutation(jax.random.fold_in(own, 3), amount)
    giver, receiver = mixed[0:amount // 2 * 2:2], mixed[1:amount // 2 * 2:2]
    margin = jnp.minimum(sizes[giver] - 1, limit - sizes[receiver]) // 2
    margin = jnp.where((giver == order[0]) | (receiver == order[0]) | (sizes[receiver] == 0), 0, jnp.maximum(margin, 0))
    shifted = jax.random.randint(jax.random.fold_in(own, 4), (amount // 2,), 0, 1 << 20) % (margin + 1)
    sizes = sizes.at[giver].add(-shifted).at[receiver].add(shifted)
    items = jnp.searchsorted(jnp.cumsum(sizes), jnp.arange(rows * top), side="right").astype(jnp.int32)
    listing = items.reshape(top, rows).T
    listing = listing[jax.random.permutation(jax.random.fold_in(own, 1), rows)]
    turn = jax.random.randint(jax.random.fold_in(own, 2), (rows, 1), 0, top)
    return jnp.take_along_axis(listing, (jnp.arange(top)[None, :] + turn) % top, axis=1)


def portions_of(amount, total, reach, lean, full):
    loads = [(1 << 20) // math.isqrt(grade ** lean) + 1 for grade in range(1, amount + 1)]
    largest = reach if full else min(reach, max(-(-total // amount), total * loads[0] // sum(loads)))
    least = 1 if total - largest >= amount - 1 else 0
    given, rest = [largest] + [least] * (amount - 1), total - largest - least * (amount - 1)
    while rest > 0:
        candidates = [i for i in range(1, amount) if given[i] < largest] or [i for i in range(1, amount) if given[i] < reach]
        pool, budget = sum([loads[i] for i in candidates]), rest
        for i in candidates:
            addition = min(reach - given[i], max(1, budget * loads[i] // pool), rest)
            given[i] = given[i] + addition
            rest = rest - addition
    return np.array(given)


def normal_values(own_key, shape, deviation, bound, cuts=(), kind=jnp.bfloat16):
    entries = deviation * jax.random.normal(own_key, shape, jnp.float32)
    if cuts:
        entries = entries * levels(own_key, shape, cuts, -0.22, 0.18)
    return jnp.clip(entries, -bound, bound).astype(kind)


def setup_inputs(seed: int = 0) -> dict:
    splits = jax.random.split(jax.random.key(seed), 8)
    tokens = normal_values(splits[0], (NCOL, COLUMN, D), 1.0, 6.0, ((0, 4), (1, 8)))
    cotangent = normal_values(splits[1], (NCOL, COLUMN, D), 1.0, 6.0, ((0, 4), (1, 8)))
    routes_keys = jax.random.split(jax.random.fold_in(splits[2], 1), NCOL * COLUMN // COLUMN)
    routes_turns = jax.random.permutation(jax.random.fold_in(splits[2], 3), NCOL * COLUMN // COLUMN)
    routes = jax.vmap(lambda own, number: routed_block(jax.random.fold_in(splits[2], 2), own, number, COLUMN, EXPERTS, TOP, CAP, 2))(routes_keys, routes_turns).reshape((NCOL, COLUMN, TOP))
    probs = jnp.clip(jnp.exp(math.log(0.3984375) - 2.5894505 * jax.random.uniform(splits[3], (NCOL, COLUMN, TOP), jnp.float32) ** levels(splits[3], (NCOL, COLUMN, TOP), ((0, 4),), -0.2, 0.2)), 0.029907227, 0.3984375).astype(jnp.bfloat16)
    w_gate = normal_values(splits[4], (EXPERTS, D, FF), D ** -0.5, 0.09375, ((0, 128), (2, 8)))
    w_up = normal_values(splits[5], (EXPERTS, D, FF), D ** -0.5, 0.09375, ((0, 128), (2, 8)))
    w_down = normal_values(splits[6], (EXPERTS, FF, D), FF ** -0.5, 0.1875, ((0, 128), (1, 8)))
    return {"tokens": tokens, "cotangent": cotangent, "routes": routes, "probs": probs, "w_gate": w_gate, "w_up": w_up, "w_down": w_down}


def column_slots(route_ids, expert_count):
    matches = (route_ids[..., None] == jnp.arange(expert_count, dtype=jnp.int32)).astype(jnp.int32)
    per_row = jnp.sum(matches, axis=-2)
    before = jnp.cumsum(per_row, axis=-2) - per_row
    return jnp.sum(matches * before[..., None, :], axis=-1).astype(jnp.int32)


def expert_pass(operands):
    expert_x, expert_grad, gate_weight, up_weight, down_weight = operands
    block_width = FF // N_DP
    gate_pre = jnp.dot(expert_x, gate_weight, preferred_element_type=jnp.float32)
    up_pre = jnp.dot(expert_x, up_weight, preferred_element_type=jnp.float32)
    sigmoid_gate = jax.nn.sigmoid(gate_pre)
    hidden = (gate_pre * sigmoid_gate * up_pre).astype(jnp.bfloat16)
    hidden_blocks = hidden.astype(jnp.float32).reshape(-1, N_DP, block_width)
    down_blocks = down_weight.astype(jnp.float32).reshape(N_DP, block_width, D)
    partial_value = jnp.einsum("sbh,bhd->bsd", hidden_blocks, down_blocks).astype(jnp.bfloat16)
    partial_value = lax.optimization_barrier(partial_value)
    expert_out = jnp.sum(partial_value.astype(jnp.float32), axis=0)
    hidden_grad = jnp.dot(expert_grad, down_weight.T, preferred_element_type=jnp.float32)
    gate_grad = (hidden_grad * up_pre * sigmoid_gate * (1.0 + gate_pre * (1.0 - sigmoid_gate))).astype(jnp.bfloat16)
    up_grad = (hidden_grad * gate_pre * sigmoid_gate).astype(jnp.bfloat16)
    gate_blocks = gate_weight.astype(jnp.float32).reshape(D, N_DP, block_width)
    up_blocks = up_weight.astype(jnp.float32).reshape(D, N_DP, block_width)
    input_part = jnp.einsum("sbh,dbh->bsd", gate_grad.astype(jnp.float32).reshape(-1, N_DP, block_width), gate_blocks)
    input_part = input_part + jnp.einsum("sbh,dbh->bsd", up_grad.astype(jnp.float32).reshape(-1, N_DP, block_width), up_blocks)
    input_part = lax.optimization_barrier(input_part.astype(jnp.bfloat16))
    expert_input = jnp.sum(input_part.astype(jnp.float32), axis=0)
    return expert_out, expert_input


def reference(tokens, cotangent, routes, probs, w_gate, w_up, w_down):
    slots = column_slots(routes, EXPERTS)
    column_ids = jnp.arange(NCOL, dtype=jnp.int32)[:, None, None]
    flat = ((routes * NCOL + column_ids) * CAP + slots).astype(jnp.int32)
    total_slots = EXPERTS * NCOL * CAP
    rows_x = jnp.broadcast_to(tokens[:, :, None, :], (NCOL, COLUMN, TOP, D)).reshape(-1, D)
    scaled = (probs.astype(jnp.float32)[..., None] * cotangent.astype(jnp.float32)[:, :, None, :]).astype(jnp.bfloat16)
    scaled = scaled.reshape(-1, D)
    expert_x = jnp.zeros((total_slots, D), jnp.bfloat16).at[flat.reshape(-1)].set(rows_x)
    expert_grad = jnp.zeros((total_slots, D), jnp.bfloat16).at[flat.reshape(-1)].set(scaled)
    expert_x = expert_x.reshape(EXPERTS, NCOL * CAP, D)
    expert_grad = expert_grad.reshape(EXPERTS, NCOL * CAP, D)
    expert_out, expert_input = lax.map(expert_pass, (expert_x, expert_grad, w_gate, w_up, w_down))
    expert_out = expert_out.reshape(total_slots, D)
    expert_input = expert_input.reshape(total_slots, D)
    mixed = jnp.sum(probs.astype(jnp.float32)[..., None] * expert_out[flat], axis=2).astype(jnp.bfloat16)
    input_grad = jnp.sum(expert_input[flat], axis=2).astype(jnp.bfloat16)
    return mixed, input_grad
```

```python
import jax
import jax.numpy as jnp
from jax import lax
from jax.sharding import PartitionSpec as P

BF16 = jnp.bfloat16
F32 = jnp.float32
ROWS = 8


def column_slots(route_ids, expert_count):
    matches = (route_ids[..., None] == jnp.arange(expert_count, dtype=jnp.int32)).astype(jnp.int32)
    per_row = jnp.sum(matches, axis=-2)
    before = jnp.cumsum(per_row, axis=-2) - per_row
    return jnp.sum(matches * before[..., None, :], axis=-1)


def contract_last(left, right):
    return lax.dot_general(
        left, right, (((1,), (1,)), ((), ())), preferred_element_type=F32
    )


def body(tokens, cotangent, routes, probs, w_gate, w_up, w_down):
    dp_count = lax.axis_size("dp")
    ctx_count = lax.axis_size("ctx")
    tp_count = lax.axis_size("tp")
    both_axes = ("ctx", "dp")
    pairs = ctx_count * dp_count
    route_ids = routes[0]
    weight = probs[0]
    column, _ = route_ids.shape
    own_rows, width = tokens.shape[1:]
    slice_width = width // dp_count
    expert_count = ctx_count * tp_count
    slot_rows = ctx_count * ROWS

    sent = jnp.concatenate((tokens[0], cotangent[0]), axis=0)
    parts = lax.all_to_all(sent, "dp", split_axis=1, concat_axis=0, tiled=True)

    slots = column_slots(route_ids, expert_count)
    owned_route = route_ids % tp_count == lax.axis_index("tp")
    position = route_ids // tp_count * ROWS + slots
    matches = (position[:, :, None] == jnp.arange(slot_rows, dtype=jnp.int32)) & owned_route[
        :, :, None
    ]
    chosen = jnp.any(matches, axis=1).astype(BF16)
    scaling = jnp.sum(
        jnp.where(matches, weight[:, :, None].astype(F32), 0.0), axis=1
    ).astype(BF16)
    kinds = jnp.stack((chosen, scaling)).reshape(2, dp_count, own_rows, ctx_count, ROWS)
    eye = jnp.eye(2, dtype=BF16)
    selector = (kinds.transpose(3, 0, 4, 1, 2)[:, :, :, :, None, :] * eye[None, :, None, None, :, None])
    selector = selector.reshape(ctx_count * 2 * ROWS, dp_count * 2 * own_rows)

    packed = jnp.dot(selector, parts, preferred_element_type=F32).astype(BF16)
    packed = jnp.broadcast_to(
        packed.reshape(ctx_count, 1, 2 * ROWS, slice_width),
        (ctx_count, dp_count, 2 * ROWS, slice_width),
    ).reshape(pairs, 2 * ROWS, slice_width)
    moved = lax.all_to_all(packed, both_axes, split_axis=0, concat_axis=0, tiled=True)
    moved = moved.reshape(ctx_count, dp_count, 2, ROWS, slice_width).transpose(2, 0, 3, 1, 4)
    expert_x, expert_dy = moved.reshape(2, slot_rows, width)

    gate_weight = w_gate[0]
    up_weight = w_up[0]
    down_weight = w_down[0]
    gate_pre = jnp.dot(expert_x, gate_weight, preferred_element_type=F32)
    up_pre = jnp.dot(expert_x, up_weight, preferred_element_type=F32)
    sigmoid_gate = jax.nn.sigmoid(gate_pre)
    hidden = (gate_pre * sigmoid_gate * up_pre).astype(BF16)
    out_term = jnp.dot(hidden, down_weight, preferred_element_type=F32)
    hidden_grad = contract_last(expert_dy, down_weight)
    gate_grad = (
        hidden_grad * up_pre * sigmoid_gate * (1.0 + gate_pre * (1.0 - sigmoid_gate))
    ).astype(BF16)
    up_grad = (hidden_grad * gate_pre * sigmoid_gate).astype(BF16)
    input_term = contract_last(gate_grad, gate_weight) + contract_last(up_grad, up_weight)

    terms = jnp.stack((out_term.astype(BF16), input_term.astype(BF16)))
    terms = terms.reshape(2, ctx_count, ROWS, dp_count, slice_width).transpose(1, 3, 0, 2, 4)
    back = lax.all_to_all(
        terms.reshape(pairs, 2 * ROWS, slice_width), both_axes, split_axis=0, concat_axis=0, tiled=True
    )
    back = jnp.sum(
        back.reshape(ctx_count, dp_count, 2, ROWS, slice_width).astype(F32), axis=1
    ).astype(BF16)
    mixed = jnp.dot(
        scaling, back[:, 0].reshape(slot_rows, slice_width), preferred_element_type=F32
    )
    grad = jnp.dot(
        chosen, back[:, 1].reshape(slot_rows, slice_width), preferred_element_type=F32
    )
    tok_rows = column // tp_count
    per_owner = jnp.stack(
        (
            mixed.astype(BF16).reshape(tp_count, tok_rows, slice_width),
            grad.astype(BF16).reshape(tp_count, tok_rows, slice_width),
        ),
        axis=1,
    ).reshape(tp_count, 2 * tok_rows, slice_width)
    got = lax.all_to_all(per_owner, "tp", split_axis=0, concat_axis=0, tiled=True)
    got = jnp.sum(got.astype(F32), axis=0).astype(BF16).reshape(2, 1, tok_rows, slice_width)
    return got[0], got[1]


def solution(mesh):
    placed = (
        P("ctx", "dp", None),
        P("ctx", "dp", None),
        P("ctx", None, None),
        P("ctx", None, None),
        P(("ctx", "tp"), None, "dp"),
        P(("ctx", "tp"), None, "dp"),
        P(("ctx", "tp"), "dp", None),
    )
    return jax.shard_map(
        body,
        mesh=mesh,
        in_specs=placed,
        out_specs=(P("ctx", "tp", "dp"), P("ctx", "tp", "dp")),
        check_vma=False,
    )
```

```python
import jax
import jax.numpy as jnp
from jax import lax
from jax.experimental import pallas as pl
from jax.experimental.pallas import tpu as pltpu
from jax.sharding import Mesh, PartitionSpec as P

BF16 = jnp.bfloat16
F32 = jnp.float32
I32 = jnp.int32
DP = ("ya", "yb")
TP = ("za", "zb", "xh")
X_PARTS = 4
CAP = 6
ROWS = 8
CUTS = 4
LANES = 128


def sixth(v):
    return (v * 10923) >> 16


def iota(shape, dim):
    return lax.broadcasted_iota(I32, shape, dim)


def dot(left, right):
    return jnp.dot(left, right, preferred_element_type=F32)


def dot_t(left, right):
    return lax.dot_general(
        left, right, (((1,), (1,)), ((), ())), preferred_element_type=F32
    )


def params(mib):
    return pltpu.CompilerParams(vmem_limit_bytes=mib << 20)


def spread_kernel(at_ref, tok_ref, cot_ref, out_ref, sems):
    own = at_ref[1]
    block = out_ref.shape[3]
    copies = []
    for d in range(out_ref.shape[0]):
        for kind, ref in enumerate((tok_ref, cot_ref)):
            start = pl.multiple_of(((d % 2) * 2 + own) * block, block)
            copies.append(
                pltpu.make_async_copy(
                    ref.at[0, :, pl.ds(start, block)], out_ref.at[d, kind], sems.at[2 * d + kind]
                )
            )
    for copy in copies:
        copy.start()
    for copy in copies:
        copy.wait()


def selector_kernel(ctx_count, tp_count, at_ref, routes_ref, probs_ref, pack_ref, mix_ref):
    za, zb, xh = at_ref[0], at_ref[1], at_ref[2]
    top, column = routes_ref.shape
    columns = 2 * column
    experts = ctx_count * tp_count
    expert = iota((experts, columns), 0).astype(F32)
    named = jnp.zeros((experts, columns), F32)
    share = jnp.zeros((experts, columns), F32)

    def token(j):
        return ((j >> 4) << 3) + (j & 7)

    def kind_of(j):
        return (j >> 3) & 1

    shape = (column, columns)
    spread = (iota(shape, 0) == token(iota(shape, 1))).astype(F32).astype(BF16)
    routes = dot(routes_ref[...].astype(F32).astype(BF16), spread)
    probs = dot(probs_ref[...], spread)
    for k in range(top):
        hit = routes[k : k + 1, :] == expert
        named = jnp.where(hit, 1.0, named)
        share = jnp.where(hit, probs[k : k + 1, :], share)

    row, col = iota((columns, columns), 0), iota((columns, columns), 1)
    earlier = ((kind_of(row) == 0) & (token(row) < token(col))).astype(F32).astype(BF16)
    named = named.astype(BF16)
    before = dot(named, earlier)
    table = jnp.concatenate((named, share.astype(BF16), before.astype(BF16)), axis=1)

    def picked(expert_rows, slot_rows):
        wanted = (expert_rows == iota(expert_rows.shape, 1)).astype(F32).astype(BF16)
        got = dot(wanted, table)
        valid = (got[:, :columns] > 0.5) & (
            got[:, 2 * columns :] == slot_rows.astype(F32)
        )
        return valid, got[:, columns : 2 * columns]

    row = iota((ctx_count * 2 * CUTS * 2 * CAP, LANES), 0)
    outer = sixth(row)
    slot = row - CAP * outer
    kind = outer & 1
    cut = (outer >> 1) & 3
    far = outer >> 3
    owner = (far >> 1) * tp_count + (za * 2 + (far & 1)) * X_PARTS + xh
    valid, scale = picked(owner, slot)
    mine = valid & (kind == kind_of(iota(row.shape, 1)))
    value = jnp.where(mine, jnp.where(kind == 1, scale, 1.0), 0.0)
    for c in range(CUTS):
        pack_ref[:, c * LANES : (c + 1) * LANES] = jnp.where(cut == c, value, 0.0).astype(BF16)

    row = iota((ctx_count * CUTS * 2 * CAP, LANES), 0)
    outer = sixth(row)
    slot = row - CAP * outer
    kind = outer & 1
    owner = (outer >> 3) * tp_count + (za * 2 + zb) * X_PARTS + xh
    valid, scale = picked(owner, slot)
    value = jnp.where(valid, jnp.where(kind == 0, scale, 1.0), 0.0).astype(BF16)
    shape = (mix_ref.shape[0], LANES)
    row, col = iota(shape, 0), iota(shape, 1)
    wanted = (kind_of(col) == 0) & (token(col) == ((row >> 4) << 1) + (row & 1))
    full = dot_t(wanted.astype(F32).astype(BF16), value)
    row, col = iota(full.shape, 0), sixth(iota(full.shape, 1))
    same = (((row >> 1) & 1) == (col & 1)) & (((row >> 2) & 3) == ((col >> 1) & 3))
    mix_ref[...] = jnp.where(same, full, 0.0).astype(BF16)


def pack_kernel(pack_ref, got_ref, out_ref):
    sources, rows, block = got_ref.shape
    got = got_ref[...].reshape(sources * rows, block)
    part = block // CUTS
    stacked = jnp.concatenate([got[:, c * part : (c + 1) * part] for c in range(CUTS)], axis=0)
    packed = dot(pack_ref[...], stacked).astype(BF16)
    size = out_ref.shape[1]
    for to in range(out_ref.shape[0]):
        c, zb = to >> 2, to & 1
        first = (c * 2 + zb) * size
        out_ref[to] = packed[first : first + size]


def expert_kernel(ctx_count, got_ref, gate_ref, up_ref, down_ref, out_ref):
    _, size, part = got_ref.shape
    blocks = got_ref.shape[0] // ctx_count
    width, hidden_rows = gate_ref.shape
    slot_rows = ctx_count * ROWS
    arrived = jnp.concatenate(
        [
            jnp.concatenate([got_ref[c * blocks + q] for q in range(blocks)], axis=1)
            for c in range(ctx_count)
        ],
        axis=0,
    )

    def source(v):
        slot, c, kind, cut = v & 7, (v >> 3) & 3, (v >> 5) & 1, v >> 6
        return jnp.where(slot < CAP, ((c * CUTS + cut) * 2 + kind) * CAP + slot, -1)

    shape = (CUTS * 2 * slot_rows, ctx_count * size)
    order = (source(iota(shape, 0)) == iota(shape, 1)).astype(F32).astype(BF16)
    sorted_rows = dot(order, arrived).astype(BF16)

    def whole(kind):
        pieces = []
        for q in range(blocks):
            for cut in range(CUTS):
                first = (cut * 2 + kind) * slot_rows
                pieces.append(sorted_rows[first : first + slot_rows, q * part : (q + 1) * part])
        return jnp.concatenate(pieces, axis=1)

    expert_x, expert_dy = whole(0), whole(1)
    gate_pre = dot(expert_x, gate_ref[...])
    up_pre = dot(expert_x, up_ref[...])
    hidden_grad = dot_t(expert_dy, down_ref[...])
    sigmoid_gate = jax.nn.sigmoid(gate_pre)
    hidden = (gate_pre * sigmoid_gate * up_pre).astype(BF16)
    gate_grad = (
        hidden_grad * up_pre * sigmoid_gate * (1.0 + gate_pre * (1.0 - sigmoid_gate))
    ).astype(BF16)
    up_grad = (hidden_grad * gate_pre * sigmoid_gate).astype(BF16)
    out_term = dot(hidden, down_ref[...]).astype(BF16)
    input_term = (dot_t(gate_grad, gate_ref[...]) + dot_t(up_grad, up_ref[...])).astype(BF16)

    dp_count = out_ref.shape[0] // ctx_count
    step = width // dp_count
    groups = []
    for cut in range(CUTS):
        for term in (out_term, input_term):
            groups.append(
                jnp.concatenate(
                    [
                        term[:, d * step + cut * LANES : d * step + (cut + 1) * LANES]
                        for d in range(dp_count)
                    ],
                    axis=1,
                )
            )
    shape = (shape[1], shape[0])
    order = (source(iota(shape, 1)) == iota(shape, 0)).astype(F32).astype(BF16)
    leaving = dot(order, jnp.concatenate(groups, axis=0)).astype(BF16)
    for c in range(ctx_count):
        for d in range(dp_count):
            out_ref[c * dp_count + d] = leaving[
                c * size : (c + 1) * size, d * LANES : (d + 1) * LANES
            ]


def combine_kernel(ctx_count, mix_ref, got_ref, out_ref):
    dp_count = got_ref.shape[0] // ctx_count
    sums = []
    for c in range(ctx_count):
        total = got_ref[c * dp_count].astype(F32)
        for d in range(1, dp_count):
            total = total + got_ref[c * dp_count + d].astype(F32)
        sums.append(total)
    rows = jnp.concatenate(sums, axis=0).astype(BF16)
    out_ref[...] = dot(mix_ref[...], rows).astype(BF16).reshape(out_ref.shape)


def finish_kernel(got_ref, mixed_ref, grad_ref):
    total = jnp.sum(got_ref[...].astype(F32), axis=0)
    count = mixed_ref.shape[0]
    for cut in range(CUTS):
        lanes = slice(cut * LANES, (cut + 1) * LANES)
        first = cut * 2 * count
        mixed_ref[:, lanes] = total[first : first + count].astype(BF16)
        grad_ref[:, lanes] = total[first + count : first + 2 * count].astype(BF16)


def body(tokens, cotangent, routes, probs, w_gate, w_up, w_down):
    dp_count = lax.axis_size("ya") * lax.axis_size("yb")
    ctx_count = lax.axis_size("ctx")
    tp_count = lax.axis_size("za") * lax.axis_size("zb") * lax.axis_size("xh")
    _, own_rows, width = tokens.shape
    column = routes.shape[1]
    block = width // 4
    size = CUTS * 2 * CAP
    tok_rows = column // tp_count
    any_space = pl.BlockSpec(memory_space=pl.ANY)
    smem = pl.BlockSpec(memory_space=pltpu.SMEM)
    vmem = pl.BlockSpec(memory_space=pltpu.VMEM)
    place = jnp.stack([lax.axis_index("za"), lax.axis_index("zb"), lax.axis_index("xh")]).astype(I32)

    spread = pl.pallas_call(
        spread_kernel,
        out_shape=jax.ShapeDtypeStruct((dp_count, 2, own_rows, block), BF16),
        in_specs=[smem, any_space, any_space],
        out_specs=any_space,
        scratch_shapes=[pltpu.SemaphoreType.DMA((2 * dp_count,))],
        compiler_params=params(4),
        name="spread",
    )(place, tokens, cotangent)
    parts = lax.all_to_all(spread, DP, split_axis=0, concat_axis=0, tiled=True)
    parts = parts.reshape(dp_count, 2 * own_rows, block)

    pack, mix = pl.pallas_call(
        lambda *refs: selector_kernel(ctx_count, tp_count, *refs),
        out_shape=(
            jax.ShapeDtypeStruct((ctx_count * 2 * size, CUTS * 2 * column), BF16),
            jax.ShapeDtypeStruct((tp_count * CUTS * 2 * tok_rows, ctx_count * size), BF16),
        ),
        in_specs=[smem, vmem, vmem],
        out_specs=(vmem, vmem),
        compiler_params=params(8),
        cost_estimate=pl.CostEstimate(flops=60_000_000, bytes_accessed=600_000, transcendentals=0),
        name="selectors",
    )(place, routes[0].T, probs[0].T)

    packed = pl.pallas_call(
        pack_kernel,
        out_shape=jax.ShapeDtypeStruct((ctx_count * 4, size, block // CUTS), BF16),
        in_specs=[vmem, vmem],
        out_specs=vmem,
        compiler_params=params(8),
        name="pack",
    )(pack, parts)
    moved = lax.all_to_all(packed, ("ctx", "yb", "zb"), split_axis=0, concat_axis=0, tiled=True)

    terms = pl.pallas_call(
        lambda *refs: expert_kernel(ctx_count, *refs),
        out_shape=jax.ShapeDtypeStruct((ctx_count * dp_count, size, LANES), BF16),
        in_specs=[vmem] * 4,
        out_specs=vmem,
        compiler_params=params(16),
        name="expert",
    )(moved, w_gate[0], w_up[0], w_down[0])
    back = lax.all_to_all(terms, ("ctx",) + DP, split_axis=0, concat_axis=0, tiled=True)

    per_owner = pl.pallas_call(
        lambda *refs: combine_kernel(ctx_count, *refs),
        out_shape=jax.ShapeDtypeStruct((tp_count, CUTS * 2 * tok_rows, LANES), BF16),
        in_specs=[vmem] * 2,
        out_specs=vmem,
        compiler_params=params(8),
        name="combine",
    )(mix, back)
    got = lax.all_to_all(per_owner, TP, split_axis=0, concat_axis=0, tiled=True)

    out = jax.ShapeDtypeStruct((tok_rows, width // dp_count), BF16)
    mixed, input_grad = pl.pallas_call(
        finish_kernel,
        out_shape=(out, out),
        in_specs=[vmem],
        out_specs=(vmem, vmem),
        compiler_params=params(4),
        name="finish",
    )(got)
    return mixed[None], input_grad[None]


def solution(mesh):
    dp_count, ctx_count, tp_count = (mesh.shape[axis] for axis in ("dp", "ctx", "tp"))
    z_count = tp_count // X_PARTS
    fine = Mesh(
        mesh.devices.reshape(dp_count // 2, 2, ctx_count, z_count // 2, 2, X_PARTS),
        ("ya", "yb", "ctx", "za", "zb", "xh"),
    )
    experts = ("ctx",) + TP
    placed = (
        P("ctx", DP, None),
        P("ctx", DP, None),
        P("ctx", None, None),
        P("ctx", None, None),
        P(experts, None, DP),
        P(experts, None, DP),
        P(experts, DP, None),
    )
    return jax.shard_map(
        body,
        mesh=fine,
        in_specs=placed,
        out_specs=(P("ctx", TP, DP), P("ctx", TP, DP)),
        check_vma=False,
    )
```

```python
import jax
import jax.numpy as jnp
from jax import lax
from jax.experimental import pallas as pl
from jax.experimental.pallas import tpu as pltpu
from jax.sharding import Mesh, PartitionSpec as P

BF16 = jnp.bfloat16
F32 = jnp.float32
I32 = jnp.int32
DP = ("ya", "yb")
TP = ("za", "zb", "xh")
X_PARTS = 4
CAP = 6
ROWS = 8
CUTS = 4
LANES = 128


def sixth(v):
    return (v * 10923) >> 16


def iota(shape, dim):
    return lax.broadcasted_iota(I32, shape, dim)


def dot(left, right):
    return jnp.dot(left, right, preferred_element_type=F32)


def dot_t(left, right):
    return lax.dot_general(
        left, right, (((1,), (1,)), ((), ())), preferred_element_type=F32
    )


def in_hbm(v):
    return pltpu.with_memory_space_constraint(v, pltpu.HBM)


def params(mib):
    return pltpu.CompilerParams(vmem_limit_bytes=mib << 20)


def spread_kernel(at_ref, tok_ref, cot_ref, out_ref, held, sems):
    own = at_ref[1]
    block = out_ref.shape[3]
    copies = []
    for yb in range(2):
        for kind, ref in enumerate((tok_ref, cot_ref)):
            start = pl.multiple_of((yb * 2 + own) * block, block)
            copies.append(
                pltpu.make_async_copy(
                    ref.at[0, :, pl.ds(start, block)], held.at[yb, kind], sems.at[2 * yb + kind]
                )
            )
    for copy in copies:
        copy.start()
    for yb in range(2):
        for kind in range(2):
            copies[2 * yb + kind].wait()
            value = held[yb, kind]
            for d in range(yb, out_ref.shape[0], 2):
                out_ref[d, kind] = value


def selector_kernel(ctx_count, tp_count, *refs):
    at_ref, routes_ref, probs_ref, *weights, pack_ref, mix_ref = refs[:8]
    copies = [
        pltpu.make_async_copy(ref.at[0], held, refs[11].at[i])
        for i, (ref, held) in enumerate(zip(weights, refs[8:11]))
    ]
    for copy in copies:
        copy.start()
    za, zb, xh = at_ref[0], at_ref[1], at_ref[2]
    top, column = routes_ref.shape
    columns = 2 * column
    experts = ctx_count * tp_count
    expert = iota((experts, columns), 0).astype(F32)
    named = jnp.zeros((experts, columns), F32)
    share = jnp.zeros((experts, columns), F32)

    def token(j):
        return ((j >> 4) << 3) + (j & 7)

    def kind_of(j):
        return (j >> 3) & 1

    shape = (column, columns)
    spread = (iota(shape, 0) == token(iota(shape, 1))).astype(F32).astype(BF16)
    routes = dot(routes_ref[...].astype(F32).astype(BF16), spread)
    probs = dot(probs_ref[...], spread)
    for k in range(top):
        hit = routes[k : k + 1, :] == expert
        named = jnp.where(hit, 1.0, named)
        share = jnp.where(hit, probs[k : k + 1, :], share)

    row, col = iota((columns, columns), 0), iota((columns, columns), 1)
    earlier = ((kind_of(row) == 0) & (token(row) < token(col))).astype(F32).astype(BF16)
    named = named.astype(BF16)
    before = dot(named, earlier)
    table = jnp.concatenate((named, share.astype(BF16), before.astype(BF16)), axis=1)

    def picked(expert_rows, slot_rows):
        wanted = (expert_rows == iota(expert_rows.shape, 1)).astype(F32).astype(BF16)
        got = dot(wanted, table)
        valid = (got[:, :columns] > 0.5) & (
            got[:, 2 * columns :] == slot_rows.astype(F32)
        )
        return valid, got[:, columns : 2 * columns]

    row = iota((ctx_count * 2 * CUTS * 2 * CAP, LANES), 0)
    outer = sixth(row)
    slot = row - CAP * outer
    kind = outer & 1
    cut = (outer >> 1) & 3
    far = outer >> 3
    owner = (far >> 1) * tp_count + (za * 2 + (far & 1)) * X_PARTS + xh
    valid, scale = picked(owner, slot)
    mine = valid & (kind == kind_of(iota(row.shape, 1)))
    value = jnp.where(mine, jnp.where(kind == 1, scale, 1.0), 0.0)
    for c in range(CUTS):
        pack_ref[:, c * LANES : (c + 1) * LANES] = jnp.where(cut == c, value, 0.0).astype(BF16)

    row = iota((ctx_count * CUTS * 2 * CAP, LANES), 0)
    outer = sixth(row)
    slot = row - CAP * outer
    kind = outer & 1
    owner = (outer >> 3) * tp_count + (za * 2 + zb) * X_PARTS + xh
    valid, scale = picked(owner, slot)
    value = jnp.where(valid, jnp.where(kind == 0, scale, 1.0), 0.0).astype(BF16)
    shape = (mix_ref.shape[0], LANES)
    row, col = iota(shape, 0), iota(shape, 1)
    wanted = (kind_of(col) == 0) & (token(col) == ((row >> 4) << 1) + (row & 1))
    full = dot_t(wanted.astype(F32).astype(BF16), value)
    row, col = iota(full.shape, 0), sixth(iota(full.shape, 1))
    same = (((row >> 1) & 1) == (col & 1)) & (((row >> 2) & 3) == ((col >> 1) & 3))
    mix_ref[...] = jnp.where(same, full, 0.0).astype(BF16)
    for copy in copies:
        copy.wait()


def pack_kernel(pack_ref, got_ref, out_ref):
    sources, rows, block = got_ref.shape
    got = got_ref[...].reshape(sources * rows, block)
    part = block // CUTS
    stacked = jnp.concatenate([got[:, c * part : (c + 1) * part] for c in range(CUTS)], axis=0)
    packed = dot(pack_ref[...], stacked).astype(BF16)
    size = out_ref.shape[1]
    for to in range(out_ref.shape[0]):
        c, zb = to >> 2, to & 1
        first = (c * 2 + zb) * size
        out_ref[to] = packed[first : first + size]


def expert_kernel(ctx_count, got_ref, gate_ref, up_ref, down_ref, out_ref):
    _, size, part = got_ref.shape
    blocks = got_ref.shape[0] // ctx_count
    width, hidden_rows = gate_ref.shape
    slot_rows = ctx_count * ROWS
    arrived = jnp.concatenate(
        [
            jnp.concatenate([got_ref[c * blocks + q] for q in range(blocks)], axis=1)
            for c in range(ctx_count)
        ],
        axis=0,
    )

    def source(v):
        slot, c, kind, cut = v & 7, (v >> 3) & 3, (v >> 5) & 1, v >> 6
        return jnp.where(slot < CAP, ((c * CUTS + cut) * 2 + kind) * CAP + slot, -1)

    shape = (CUTS * 2 * slot_rows, ctx_count * size)
    order = (source(iota(shape, 0)) == iota(shape, 1)).astype(F32).astype(BF16)
    sorted_rows = dot(order, arrived).astype(BF16)

    def whole(kind):
        pieces = []
        for q in range(blocks):
            for cut in range(CUTS):
                first = (cut * 2 + kind) * slot_rows
                pieces.append(sorted_rows[first : first + slot_rows, q * part : (q + 1) * part])
        return jnp.concatenate(pieces, axis=1)

    expert_x, expert_dy = whole(0), whole(1)
    gate_pre = dot(expert_x, gate_ref[...])
    up_pre = dot(expert_x, up_ref[...])
    hidden_grad = dot_t(expert_dy, down_ref[...])
    sigmoid_gate = jax.nn.sigmoid(gate_pre)
    hidden = (gate_pre * sigmoid_gate * up_pre).astype(BF16)
    gate_grad = (
        hidden_grad * up_pre * sigmoid_gate * (1.0 + gate_pre * (1.0 - sigmoid_gate))
    ).astype(BF16)
    up_grad = (hidden_grad * gate_pre * sigmoid_gate).astype(BF16)
    out_term = dot(hidden, down_ref[...]).astype(BF16)
    input_term = (dot_t(gate_grad, gate_ref[...]) + dot_t(up_grad, up_ref[...])).astype(BF16)

    dp_count = out_ref.shape[0] // ctx_count
    step = width // dp_count
    groups = []
    for cut in range(CUTS):
        for term in (out_term, input_term):
            groups.append(
                jnp.concatenate(
                    [
                        term[:, d * step + cut * LANES : d * step + (cut + 1) * LANES]
                        for d in range(dp_count)
                    ],
                    axis=1,
                )
            )
    shape = (shape[1], shape[0])
    order = (source(iota(shape, 1)) == iota(shape, 0)).astype(F32).astype(BF16)
    leaving = dot(order, jnp.concatenate(groups, axis=0)).astype(BF16)
    for c in range(ctx_count):
        for d in range(dp_count):
            out_ref[c * dp_count + d] = leaving[
                c * size : (c + 1) * size, d * LANES : (d + 1) * LANES
            ]


def combine_kernel(ctx_count, mix_ref, got_ref, out_ref):
    dp_count = got_ref.shape[0] // ctx_count
    sums = []
    for c in range(ctx_count):
        total = got_ref[c * dp_count].astype(F32)
        for d in range(1, dp_count):
            total = total + got_ref[c * dp_count + d].astype(F32)
        sums.append(total)
    rows = jnp.concatenate(sums, axis=0).astype(BF16)
    out_ref[...] = dot(mix_ref[...], rows).astype(BF16).reshape(out_ref.shape)


def finish_kernel(got_ref, mixed_ref, grad_ref):
    total = jnp.sum(got_ref[...].astype(F32), axis=0)
    count = mixed_ref.shape[0]
    for cut in range(CUTS):
        lanes = slice(cut * LANES, (cut + 1) * LANES)
        first = cut * 2 * count
        mixed_ref[:, lanes] = total[first : first + count].astype(BF16)
        grad_ref[:, lanes] = total[first + count : first + 2 * count].astype(BF16)


def body(tokens, cotangent, routes, probs, w_gate, w_up, w_down):
    dp_count = lax.axis_size("ya") * lax.axis_size("yb")
    ctx_count = lax.axis_size("ctx")
    tp_count = lax.axis_size("za") * lax.axis_size("zb") * lax.axis_size("xh")
    _, own_rows, width = tokens.shape
    column = routes.shape[1]
    block = width // 4
    size = CUTS * 2 * CAP
    tok_rows = column // tp_count
    any_space = pl.BlockSpec(memory_space=pl.ANY)
    smem = pl.BlockSpec(memory_space=pltpu.SMEM)
    vmem = pl.BlockSpec(memory_space=pltpu.VMEM)
    place = jnp.stack([lax.axis_index("za"), lax.axis_index("zb"), lax.axis_index("xh")]).astype(I32)

    spread = pl.pallas_call(
        spread_kernel,
        out_shape=pltpu.VMEM((dp_count, 2, own_rows, block), BF16),
        in_specs=[smem, any_space, any_space],
        out_specs=vmem,
        scratch_shapes=[
            pltpu.VMEM((2, 2, own_rows, block), BF16),
            pltpu.SemaphoreType.DMA((4,)),
        ],
        compiler_params=params(4),
        name="spread",
    )(place, in_hbm(tokens), in_hbm(cotangent))
    parts = lax.all_to_all(spread, DP, split_axis=0, concat_axis=0, tiled=True)
    parts = parts.reshape(dp_count, 2 * own_rows, block)

    weights = (w_gate, w_up, w_down)
    pack, mix, *held = pl.pallas_call(
        lambda *refs: selector_kernel(ctx_count, tp_count, *refs),
        out_shape=(
            jax.ShapeDtypeStruct((ctx_count * 2 * size, CUTS * 2 * column), BF16),
            jax.ShapeDtypeStruct((tp_count * CUTS * 2 * tok_rows, ctx_count * size), BF16),
            *(pltpu.VMEM(weight.shape[1:], BF16) for weight in weights),
        ),
        in_specs=[smem, vmem, vmem] + [any_space] * 3,
        out_specs=(vmem,) * 5,
        scratch_shapes=[pltpu.SemaphoreType.DMA((3,))],
        compiler_params=params(8),
        cost_estimate=pl.CostEstimate(flops=60_000_000, bytes_accessed=7_000_000, transcendentals=0),
        name="selectors",
    )(place, routes[0].T, probs[0].T, *(in_hbm(weight) for weight in weights))

    packed = pl.pallas_call(
        pack_kernel,
        out_shape=jax.ShapeDtypeStruct((ctx_count * 4, size, block // CUTS), BF16),
        in_specs=[vmem, vmem],
        out_specs=vmem,
        compiler_params=params(8),
        name="pack",
    )(pack, parts)
    moved = lax.all_to_all(packed, ("ctx", "yb", "zb"), split_axis=0, concat_axis=0, tiled=True)

    terms = pl.pallas_call(
        lambda *refs: expert_kernel(ctx_count, *refs),
        out_shape=jax.ShapeDtypeStruct((ctx_count * dp_count, size, LANES), BF16),
        in_specs=[vmem] * 4,
        out_specs=vmem,
        compiler_params=params(16),
        name="expert",
    )(moved, *held)
    back = lax.all_to_all(terms, ("ctx",) + DP, split_axis=0, concat_axis=0, tiled=True)

    per_owner = pl.pallas_call(
        lambda *refs: combine_kernel(ctx_count, *refs),
        out_shape=jax.ShapeDtypeStruct((tp_count, CUTS * 2 * tok_rows, LANES), BF16),
        in_specs=[vmem] * 2,
        out_specs=vmem,
        compiler_params=params(8),
        name="combine",
    )(mix, back)
    got = lax.all_to_all(per_owner, TP, split_axis=0, concat_axis=0, tiled=True)

    out = jax.ShapeDtypeStruct((tok_rows, width // dp_count), BF16)
    mixed, input_grad = pl.pallas_call(
        finish_kernel,
        out_shape=(out, out),
        in_specs=[vmem],
        out_specs=(vmem, vmem),
        compiler_params=params(4),
        name="finish",
    )(got)
    return mixed[None], input_grad[None]


def solution(mesh):
    dp_count, ctx_count, tp_count = (mesh.shape[axis] for axis in ("dp", "ctx", "tp"))
    z_count = tp_count // X_PARTS
    fine = Mesh(
        mesh.devices.reshape(dp_count // 2, 2, ctx_count, z_count // 2, 2, X_PARTS),
        ("ya", "yb", "ctx", "za", "zb", "xh"),
    )
    experts = ("ctx",) + TP
    placed = (
        P("ctx", DP, None),
        P("ctx", DP, None),
        P("ctx", None, None),
        P("ctx", None, None),
        P(experts, None, DP),
        P(experts, None, DP),
        P(experts, DP, None),
    )
    return jax.shard_map(
        body,
        mesh=fine,
        in_specs=placed,
        out_specs=(P("ctx", TP, DP), P("ctx", TP, DP)),
        check_vma=False,
    )
```

```python
import jax
import jax.numpy as jnp
from jax import lax
from jax.experimental import pallas as pl
from jax.experimental.pallas import tpu as pltpu
from jax.sharding import Mesh, PartitionSpec as P

BF16 = jnp.bfloat16
F32 = jnp.float32
I32 = jnp.int32
DP = ("ya", "yb")
TP = ("za", "zb", "xh")
X_PARTS = 4
CAP = 6
ROWS = 8
CUTS = 4
LANES = 128


def sixth(v):
    return (v * 10923) >> 16


def iota(shape, dim):
    return lax.broadcasted_iota(I32, shape, dim)


def dot(left, right):
    return jnp.dot(left, right, preferred_element_type=F32)


def dot_t(left, right):
    return lax.dot_general(
        left, right, (((1,), (1,)), ((), ())), preferred_element_type=F32
    )


def in_hbm(v):
    return pltpu.with_memory_space_constraint(v, pltpu.HBM)


def params(mib):
    return pltpu.CompilerParams(vmem_limit_bytes=mib << 20)


def selectors(ctx_count, tp_count, place, routes_ref, probs_ref, pack_ref, mix_ref):
    za, zb, xh = place
    top, column = routes_ref.shape
    columns = 2 * column
    experts = ctx_count * tp_count
    expert = iota((experts, columns), 0).astype(F32)
    named = jnp.zeros((experts, columns), F32)
    share = jnp.zeros((experts, columns), F32)

    def token(j):
        return ((j >> 4) << 3) + (j & 7)

    def kind_of(j):
        return (j >> 3) & 1

    shape = (column, columns)
    spread = (iota(shape, 0) == token(iota(shape, 1))).astype(F32).astype(BF16)
    routes = dot(routes_ref[...].astype(F32).astype(BF16), spread)
    probs = dot(probs_ref[...], spread)
    for k in range(top):
        hit = routes[k : k + 1, :] == expert
        named = jnp.where(hit, 1.0, named)
        share = jnp.where(hit, probs[k : k + 1, :], share)

    row, col = iota((columns, columns), 0), iota((columns, columns), 1)
    earlier = ((kind_of(row) == 0) & (token(row) < token(col))).astype(F32).astype(BF16)
    named = named.astype(BF16)
    before = dot(named, earlier)
    table = jnp.concatenate((named, share.astype(BF16), before.astype(BF16)), axis=1)

    def picked(expert_rows, slot_rows):
        wanted = (expert_rows == iota(expert_rows.shape, 1)).astype(F32).astype(BF16)
        got = dot(wanted, table)
        valid = (got[:, :columns] > 0.5) & (
            got[:, 2 * columns :] == slot_rows.astype(F32)
        )
        return valid, got[:, columns : 2 * columns]

    row = iota((ctx_count * 2 * CUTS * 2 * CAP, LANES), 0)
    outer = sixth(row)
    slot = row - CAP * outer
    kind = outer & 1
    cut = (outer >> 1) & 3
    far = outer >> 3
    owner = (far >> 1) * tp_count + (za * 2 + (far & 1)) * X_PARTS + xh
    valid, scale = picked(owner, slot)
    mine = valid & (kind == kind_of(iota(row.shape, 1)))
    value = jnp.where(mine, jnp.where(kind == 1, scale, 1.0), 0.0)
    for c in range(CUTS):
        pack_ref[:, c * LANES : (c + 1) * LANES] = jnp.where(cut == c, value, 0.0).astype(BF16)

    row = iota((ctx_count * CUTS * 2 * CAP, LANES), 0)
    outer = sixth(row)
    slot = row - CAP * outer
    kind = outer & 1
    owner = (outer >> 3) * tp_count + (za * 2 + zb) * X_PARTS + xh
    valid, scale = picked(owner, slot)
    value = jnp.where(valid, jnp.where(kind == 0, scale, 1.0), 0.0).astype(BF16)
    shape = (mix_ref.shape[0], LANES)
    row, col = iota(shape, 0), iota(shape, 1)
    wanted = (kind_of(col) == 0) & (token(col) == ((row >> 4) << 1) + (row & 1))
    full = dot_t(wanted.astype(F32).astype(BF16), value)
    row, col = iota(full.shape, 0), sixth(iota(full.shape, 1))
    same = (((row >> 1) & 1) == (col & 1)) & (((row >> 2) & 3) == ((col >> 1) & 3))
    mix_ref[...] = jnp.where(same, full, 0.0).astype(BF16)


def first_kernel(
    ctx_count, tp_count, tok_ref, cot_ref, routes_ref, probs_ref, weight_ref,
    out_ref, pack_ref, mix_ref, weight_out, held, routes, probs, sems,
):
    za, zb, xh = (lax.axis_index(axis) for axis in TP)
    block = out_ref.shape[3]
    small = [
        pltpu.make_async_copy(ref, to, sems.at[4 + i])
        for i, (ref, to) in enumerate(((routes_ref, routes), (probs_ref, probs)))
    ]
    copies = []
    for yb in range(2):
        for kind, ref in enumerate((tok_ref, cot_ref)):
            start = pl.multiple_of((yb * 2 + zb) * block, block)
            copies.append(
                pltpu.make_async_copy(
                    ref.at[0, :, pl.ds(start, block)], held.at[yb, kind], sems.at[2 * yb + kind]
                )
            )
    weight_copy = pltpu.make_async_copy(weight_ref.at[0], weight_out, sems.at[6])
    for copy in small + copies + [weight_copy]:
        copy.start()
    for copy in small:
        copy.wait()
    selectors(ctx_count, tp_count, (za, zb, xh), routes, probs, pack_ref, mix_ref)
    for yb in range(2):
        for kind in range(2):
            copies[2 * yb + kind].wait()
            value = held[yb, kind]
            for d in range(yb, out_ref.shape[0], 2):
                out_ref[d, kind] = value
    weight_copy.wait()


def pack_kernel(pack_ref, got_ref, out_ref):
    sources, rows, block = got_ref.shape
    got = got_ref[...].reshape(sources * rows, block)
    part = block // CUTS
    stacked = jnp.concatenate([got[:, c * part : (c + 1) * part] for c in range(CUTS)], axis=0)
    packed = dot(pack_ref[...], stacked).astype(BF16)
    size = out_ref.shape[1]
    for to in range(out_ref.shape[0]):
        c, zb = to >> 2, to & 1
        first = (c * 2 + zb) * size
        out_ref[to] = packed[first : first + size]


def expert_kernel(ctx_count, got_ref, gate_ref, up_ref, down_ref, out_ref):
    _, size, part = got_ref.shape
    blocks = got_ref.shape[0] // ctx_count
    width, hidden_rows = gate_ref.shape
    slot_rows = ctx_count * ROWS
    arrived = jnp.concatenate(
        [
            jnp.concatenate([got_ref[c * blocks + q] for q in range(blocks)], axis=1)
            for c in range(ctx_count)
        ],
        axis=0,
    )

    def source(v):
        slot, c, kind, cut = v & 7, (v >> 3) & 3, (v >> 5) & 1, v >> 6
        return jnp.where(slot < CAP, ((c * CUTS + cut) * 2 + kind) * CAP + slot, -1)

    shape = (CUTS * 2 * slot_rows, ctx_count * size)
    order = (source(iota(shape, 0)) == iota(shape, 1)).astype(F32).astype(BF16)
    sorted_rows = dot(order, arrived).astype(BF16)

    def whole(kind):
        pieces = []
        for q in range(blocks):
            for cut in range(CUTS):
                first = (cut * 2 + kind) * slot_rows
                pieces.append(sorted_rows[first : first + slot_rows, q * part : (q + 1) * part])
        return jnp.concatenate(pieces, axis=1)

    expert_x, expert_dy = whole(0), whole(1)
    gate_pre = dot(expert_x, gate_ref[...])
    up_pre = dot(expert_x, up_ref[...])
    hidden_grad = dot_t(expert_dy, down_ref[...])
    sigmoid_gate = jax.nn.sigmoid(gate_pre)
    hidden = (gate_pre * sigmoid_gate * up_pre).astype(BF16)
    gate_grad = (
        hidden_grad * up_pre * sigmoid_gate * (1.0 + gate_pre * (1.0 - sigmoid_gate))
    ).astype(BF16)
    up_grad = (hidden_grad * gate_pre * sigmoid_gate).astype(BF16)
    out_term = dot(hidden, down_ref[...]).astype(BF16)
    input_term = (dot_t(gate_grad, gate_ref[...]) + dot_t(up_grad, up_ref[...])).astype(BF16)

    dp_count = out_ref.shape[0] // ctx_count
    step = width // dp_count
    groups = []
    for cut in range(CUTS):
        for term in (out_term, input_term):
            groups.append(
                jnp.concatenate(
                    [
                        term[:, d * step + cut * LANES : d * step + (cut + 1) * LANES]
                        for d in range(dp_count)
                    ],
                    axis=1,
                )
            )
    shape = (shape[1], shape[0])
    order = (source(iota(shape, 1)) == iota(shape, 0)).astype(F32).astype(BF16)
    leaving = dot(order, jnp.concatenate(groups, axis=0)).astype(BF16)
    for c in range(ctx_count):
        for d in range(dp_count):
            out_ref[c * dp_count + d] = leaving[
                c * size : (c + 1) * size, d * LANES : (d + 1) * LANES
            ]


def combine_kernel(ctx_count, mix_ref, got_ref, out_ref):
    dp_count = got_ref.shape[0] // ctx_count
    sums = []
    for c in range(ctx_count):
        total = got_ref[c * dp_count].astype(F32)
        for d in range(1, dp_count):
            total = total + got_ref[c * dp_count + d].astype(F32)
        sums.append(total)
    rows = jnp.concatenate(sums, axis=0).astype(BF16)
    out_ref[...] = dot(mix_ref[...], rows).astype(BF16).reshape(out_ref.shape)


def finish_kernel(got_ref, mixed_ref, grad_ref):
    total = jnp.sum(got_ref[...].astype(F32), axis=0)
    count = mixed_ref.shape[0]
    for cut in range(CUTS):
        lanes = slice(cut * LANES, (cut + 1) * LANES)
        first = cut * 2 * count
        mixed_ref[:, lanes] = total[first : first + count].astype(BF16)
        grad_ref[:, lanes] = total[first + count : first + 2 * count].astype(BF16)


def body(tokens, cotangent, routes, probs, w_gate, w_up, w_down):
    dp_count = lax.axis_size("ya") * lax.axis_size("yb")
    ctx_count = lax.axis_size("ctx")
    tp_count = lax.axis_size("za") * lax.axis_size("zb") * lax.axis_size("xh")
    _, own_rows, width = tokens.shape
    column, top = routes.shape[1:]
    block = width // 4
    size = CUTS * 2 * CAP
    tok_rows = column // tp_count
    any_space = pl.BlockSpec(memory_space=pl.ANY)
    vmem = pl.BlockSpec(memory_space=pltpu.VMEM)

    spread, pack, mix, down = pl.pallas_call(
        lambda *refs: first_kernel(ctx_count, tp_count, *refs),
        out_shape=(
            pltpu.VMEM((dp_count, 2, own_rows, block), BF16),
            pltpu.VMEM((ctx_count * 2 * size, CUTS * 2 * column), BF16),
            pltpu.VMEM((tp_count * CUTS * 2 * tok_rows, ctx_count * size), BF16),
            pltpu.VMEM(w_down.shape[1:], BF16),
        ),
        in_specs=[any_space] * 5,
        out_specs=(vmem,) * 4,
        scratch_shapes=[
            pltpu.VMEM((2, 2, own_rows, block), BF16),
            pltpu.VMEM((top, column), I32),
            pltpu.VMEM((top, column), BF16),
            pltpu.SemaphoreType.DMA((7,)),
        ],
        compiler_params=params(8),
        name="first",
    )(*(in_hbm(v) for v in (tokens, cotangent, routes[0].T, probs[0].T, w_down)))
    parts = lax.all_to_all(spread, DP, split_axis=0, concat_axis=0, tiled=True)
    parts = parts.reshape(dp_count, 2 * own_rows, block)

    packed = pl.pallas_call(
        pack_kernel,
        out_shape=jax.ShapeDtypeStruct((ctx_count * 4, size, block // CUTS), BF16),
        in_specs=[vmem, vmem],
        out_specs=vmem,
        compiler_params=params(8),
        name="pack",
    )(pack, parts)
    moved = lax.all_to_all(packed, ("ctx", "yb", "zb"), split_axis=0, concat_axis=0, tiled=True)

    terms = pl.pallas_call(
        lambda *refs: expert_kernel(ctx_count, *refs),
        out_shape=jax.ShapeDtypeStruct((ctx_count * dp_count, size, LANES), BF16),
        in_specs=[vmem] * 4,
        out_specs=vmem,
        compiler_params=params(16),
        name="expert",
    )(moved, w_gate[0], w_up[0], down)
    back = lax.all_to_all(terms, ("ctx",) + DP, split_axis=0, concat_axis=0, tiled=True)

    per_owner = pl.pallas_call(
        lambda *refs: combine_kernel(ctx_count, *refs),
        out_shape=jax.ShapeDtypeStruct((tp_count, CUTS * 2 * tok_rows, LANES), BF16),
        in_specs=[vmem] * 2,
        out_specs=vmem,
        compiler_params=params(8),
        name="combine",
    )(mix, back)
    got = lax.all_to_all(per_owner, TP, split_axis=0, concat_axis=0, tiled=True)

    out = jax.ShapeDtypeStruct((tok_rows, width // dp_count), BF16)
    mixed, input_grad = pl.pallas_call(
        finish_kernel,
        out_shape=(out, out),
        in_specs=[vmem],
        out_specs=(vmem, vmem),
        compiler_params=params(4),
        name="finish",
    )(got)
    return mixed[None], input_grad[None]


def solution(mesh):
    dp_count, ctx_count, tp_count = (mesh.shape[axis] for axis in ("dp", "ctx", "tp"))
    z_count = tp_count // X_PARTS
    fine = Mesh(
        mesh.devices.reshape(dp_count // 2, 2, ctx_count, z_count // 2, 2, X_PARTS),
        ("ya", "yb", "ctx", "za", "zb", "xh"),
    )
    experts = ("ctx",) + TP
    placed = (
        P("ctx", DP, None),
        P("ctx", DP, None),
        P("ctx", None, None),
        P("ctx", None, None),
        P(experts, None, DP),
        P(experts, None, DP),
        P(experts, DP, None),
    )
    return jax.shard_map(
        body,
        mesh=fine,
        in_specs=placed,
        out_specs=(P("ctx", TP, DP), P("ctx", TP, DP)),
        check_vma=False,
    )
```

```python
import jax
import jax.numpy as jnp
from jax import lax
from jax.experimental import pallas as pl
from jax.experimental.pallas import tpu as pltpu
from jax.sharding import Mesh, PartitionSpec as P

BF16 = jnp.bfloat16
F32 = jnp.float32
I32 = jnp.int32
DP = ("ya", "yb")
TP = ("za", "zb", "xh")
X_PARTS = 4
CAP = 6
ROWS = 8
CUTS = 4
LANES = 128


def order_of(count, first):
    return [(first + i) % count for i in range(count)]


def exchange(v, axes, order):
    return lax.all_to_all(
        v, axes, split_axis=0, concat_axis=0, axis_index_groups=[order], tiled=True
    )


def sixth(v):
    return (v * 10923) >> 16


def iota(shape, dim):
    return lax.broadcasted_iota(I32, shape, dim)


def dot(left, right):
    return jnp.dot(left, right, preferred_element_type=F32)


def dot_t(left, right):
    return lax.dot_general(
        left, right, (((1,), (1,)), ((), ())), preferred_element_type=F32
    )


def in_hbm(v):
    return pltpu.with_memory_space_constraint(v, pltpu.HBM)


def params(mib):
    return pltpu.CompilerParams(vmem_limit_bytes=mib << 20)


def selectors(ctx_count, tp_count, place, routes_ref, probs_ref, pack_ref, mix_ref):
    za, zb, xh = place
    top, column = routes_ref.shape
    columns = 2 * column
    experts = ctx_count * tp_count
    expert = iota((experts, columns), 0).astype(F32)
    named = jnp.zeros((experts, columns), F32)
    share = jnp.zeros((experts, columns), F32)

    def token(j):
        return ((j >> 4) << 3) + (j & 7)

    def kind_of(j):
        return (j >> 3) & 1

    shape = (column, columns)
    spread = (iota(shape, 0) == token(iota(shape, 1))).astype(F32).astype(BF16)
    routes = dot(routes_ref[...].astype(F32).astype(BF16), spread)
    probs = dot(probs_ref[...], spread)
    for k in range(top):
        hit = routes[k : k + 1, :] == expert
        named = jnp.where(hit, 1.0, named)
        share = jnp.where(hit, probs[k : k + 1, :], share)

    row, col = iota((columns, columns), 0), iota((columns, columns), 1)
    earlier = ((kind_of(row) == 0) & (token(row) < token(col))).astype(F32).astype(BF16)
    named = named.astype(BF16)
    before = dot(named, earlier)
    table = jnp.concatenate((named, share.astype(BF16), before.astype(BF16)), axis=1)

    def picked(expert_rows, slot_rows):
        wanted = (expert_rows == iota(expert_rows.shape, 1)).astype(F32).astype(BF16)
        got = dot(wanted, table)
        valid = (got[:, :columns] > 0.5) & (
            got[:, 2 * columns :] == slot_rows.astype(F32)
        )
        return valid, got[:, columns : 2 * columns]

    row = iota((ctx_count * 2 * CUTS * 2 * CAP, LANES), 0)
    outer = sixth(row)
    slot = row - CAP * outer
    kind = outer & 1
    cut = (outer >> 1) & 3
    far = outer >> 3
    owner = (far >> 1) * tp_count + (za * 2 + (far & 1)) * X_PARTS + xh
    valid, scale = picked(owner, slot)
    mine = valid & (kind == kind_of(iota(row.shape, 1)))
    value = jnp.where(mine, jnp.where(kind == 1, scale, 1.0), 0.0)
    for c in range(CUTS):
        pack_ref[:, c * LANES : (c + 1) * LANES] = jnp.where(cut == c, value, 0.0).astype(BF16)

    row = iota((ctx_count * CUTS * 2 * CAP, LANES), 0)
    outer = sixth(row)
    slot = row - CAP * outer
    kind = outer & 1
    owner = (outer >> 3) * tp_count + (za * 2 + zb) * X_PARTS + xh
    valid, scale = picked(owner, slot)
    value = jnp.where(valid, jnp.where(kind == 0, scale, 1.0), 0.0).astype(BF16)
    shape = (mix_ref.shape[0], LANES)
    row, col = iota(shape, 0), iota(shape, 1)
    wanted = (kind_of(col) == 0) & (token(col) == ((row >> 4) << 1) + (row & 1))
    full = dot_t(wanted.astype(F32).astype(BF16), value)
    row, col = iota(full.shape, 0), sixth(iota(full.shape, 1))
    same = (((row >> 1) & 1) == (col & 1)) & (((row >> 2) & 3) == ((col >> 1) & 3))
    mix_ref[...] = jnp.where(same, full, 0.0).astype(BF16)


def first_kernel(
    ctx_count, tp_count, order, tok_ref, cot_ref, routes_ref, probs_ref, weight_ref,
    out_ref, pack_ref, mix_ref, weight_out, held, routes, probs, sems,
):
    za, zb, xh = (lax.axis_index(axis) for axis in TP)
    block = out_ref.shape[3]
    small = [
        pltpu.make_async_copy(ref, to, sems.at[4 + i])
        for i, (ref, to) in enumerate(((routes_ref, routes), (probs_ref, probs)))
    ]
    copies = []
    for yb in range(2):
        for kind, ref in enumerate((tok_ref, cot_ref)):
            start = pl.multiple_of((yb * 2 + zb) * block, block)
            copies.append(
                pltpu.make_async_copy(
                    ref.at[0, :, pl.ds(start, block)], held.at[yb, kind], sems.at[2 * yb + kind]
                )
            )
    weight_copy = pltpu.make_async_copy(weight_ref.at[0], weight_out, sems.at[6])
    for copy in small + copies + [weight_copy]:
        copy.start()
    for copy in small:
        copy.wait()
    selectors(ctx_count, tp_count, (za, zb, xh), routes, probs, pack_ref, mix_ref)
    for yb in range(2):
        for kind in range(2):
            copies[2 * yb + kind].wait()
            value = held[yb, kind]
            for place, d in enumerate(order):
                if d % 2 == yb:
                    out_ref[place, kind] = value
    weight_copy.wait()


def pack_kernel(order_in, order_out, pack_ref, got_ref, out_ref):
    sources, rows, block = got_ref.shape
    got = jnp.concatenate([got_ref[order_in.index(d)] for d in range(sources)], axis=0)
    part = block // CUTS
    stacked = jnp.concatenate([got[:, c * part : (c + 1) * part] for c in range(CUTS)], axis=0)
    packed = dot(pack_ref[...], stacked).astype(BF16)
    size = out_ref.shape[1]
    for place, to in enumerate(order_out):
        c, zb = to >> 2, to & 1
        first = (c * 2 + zb) * size
        out_ref[place] = packed[first : first + size]


def expert_kernel(ctx_count, order_in, order_out, got_ref, gate_ref, up_ref, down_ref, out_ref):
    _, size, part = got_ref.shape
    blocks = got_ref.shape[0] // ctx_count
    width, hidden_rows = gate_ref.shape
    slot_rows = ctx_count * ROWS
    arrived = jnp.concatenate(
        [
            jnp.concatenate([got_ref[order_in.index(c * blocks + q)] for q in range(blocks)], axis=1)
            for c in range(ctx_count)
        ],
        axis=0,
    )

    def source(v):
        slot, c, kind, cut = v & 7, (v >> 3) & 3, (v >> 5) & 1, v >> 6
        return jnp.where(slot < CAP, ((c * CUTS + cut) * 2 + kind) * CAP + slot, -1)

    shape = (CUTS * 2 * slot_rows, ctx_count * size)
    order = (source(iota(shape, 0)) == iota(shape, 1)).astype(F32).astype(BF16)
    sorted_rows = dot(order, arrived).astype(BF16)

    def whole(kind):
        pieces = []
        for q in range(blocks):
            for cut in range(CUTS):
                first = (cut * 2 + kind) * slot_rows
                pieces.append(sorted_rows[first : first + slot_rows, q * part : (q + 1) * part])
        return jnp.concatenate(pieces, axis=1)

    expert_x, expert_dy = whole(0), whole(1)
    into = jnp.concatenate((gate_ref[...], up_ref[...]), axis=1)
    pre = dot(expert_x, into)
    gate_pre, up_pre = pre[:, :hidden_rows], pre[:, hidden_rows:]
    hidden_grad = dot_t(down_ref[...], expert_dy).T
    sigmoid_gate = jax.nn.sigmoid(gate_pre)
    hidden = (gate_pre * sigmoid_gate * up_pre).astype(BF16)
    gate_grad = (
        hidden_grad * up_pre * sigmoid_gate * (1.0 + gate_pre * (1.0 - sigmoid_gate))
    ).astype(BF16)
    up_grad = (hidden_grad * gate_pre * sigmoid_gate).astype(BF16)
    out_term = dot(hidden, down_ref[...]).astype(BF16)
    input_term = dot_t(jnp.concatenate((gate_grad, up_grad), axis=1), into).astype(BF16)

    dp_count = out_ref.shape[0] // ctx_count
    step = width // dp_count
    groups = []
    for cut in range(CUTS):
        for term in (out_term, input_term):
            groups.append(
                jnp.concatenate(
                    [
                        term[:, d * step + cut * LANES : d * step + (cut + 1) * LANES]
                        for d in range(dp_count)
                    ],
                    axis=1,
                )
            )
    shape = (shape[1], shape[0])
    order = (source(iota(shape, 1)) == iota(shape, 0)).astype(F32).astype(BF16)
    leaving = dot(order, jnp.concatenate(groups, axis=0)).astype(BF16)
    for place, to in enumerate(order_out):
        c, d = to // dp_count, to % dp_count
        out_ref[place] = leaving[c * size : (c + 1) * size, d * LANES : (d + 1) * LANES]


def combine_kernel(ctx_count, order_in, order_out, mix_ref, got_ref, out_ref):
    dp_count = got_ref.shape[0] // ctx_count
    sums = []
    for c in range(ctx_count):
        total = got_ref[order_in.index(c * dp_count)].astype(F32)
        for d in range(1, dp_count):
            total = total + got_ref[order_in.index(c * dp_count + d)].astype(F32)
        sums.append(total)
    rows = jnp.concatenate(sums, axis=0).astype(BF16)
    mixed = dot(mix_ref[...], rows).astype(BF16).reshape(out_ref.shape)
    for place, to in enumerate(order_out):
        out_ref[place] = mixed[to]


def finish_kernel(got_ref, mixed_ref, grad_ref):
    total = jnp.sum(got_ref[...].astype(F32), axis=0)
    count = mixed_ref.shape[0]
    for cut in range(CUTS):
        lanes = slice(cut * LANES, (cut + 1) * LANES)
        first = cut * 2 * count
        mixed_ref[:, lanes] = total[first : first + count].astype(BF16)
        grad_ref[:, lanes] = total[first + count : first + 2 * count].astype(BF16)


def body(tokens, cotangent, routes, probs, w_gate, w_up, w_down):
    dp_count = lax.axis_size("ya") * lax.axis_size("yb")
    ctx_count = lax.axis_size("ctx")
    tp_count = lax.axis_size("za") * lax.axis_size("zb") * lax.axis_size("xh")
    _, own_rows, width = tokens.shape
    column, top = routes.shape[1:]
    orders = (
        order_of(dp_count, 4),
        order_of(ctx_count * 4, 1),
        order_of(ctx_count * dp_count, 4),
        order_of(tp_count, 30),
    )
    block = width // 4
    size = CUTS * 2 * CAP
    tok_rows = column // tp_count
    any_space = pl.BlockSpec(memory_space=pl.ANY)
    vmem = pl.BlockSpec(memory_space=pltpu.VMEM)

    spread, pack, mix, down = pl.pallas_call(
        lambda *refs: first_kernel(ctx_count, tp_count, orders[0], *refs),
        out_shape=(
            pltpu.VMEM((dp_count, 2, own_rows, block), BF16),
            pltpu.VMEM((ctx_count * 2 * size, CUTS * 2 * column), BF16),
            pltpu.VMEM((tp_count * CUTS * 2 * tok_rows, ctx_count * size), BF16),
            pltpu.VMEM(w_down.shape[1:], BF16),
        ),
        in_specs=[any_space] * 5,
        out_specs=(vmem,) * 4,
        scratch_shapes=[
            pltpu.VMEM((2, 2, own_rows, block), BF16),
            pltpu.VMEM((top, column), I32),
            pltpu.VMEM((top, column), BF16),
            pltpu.SemaphoreType.DMA((7,)),
        ],
        compiler_params=params(8),
        name="first",
    )(*(in_hbm(v) for v in (tokens, cotangent, routes[0].T, probs[0].T, w_down)))
    parts = exchange(spread, DP, orders[0])
    parts = parts.reshape(dp_count, 2 * own_rows, block)

    packed = pl.pallas_call(
        lambda *refs: pack_kernel(orders[0], orders[1], *refs),
        out_shape=jax.ShapeDtypeStruct((ctx_count * 4, size, block // CUTS), BF16),
        in_specs=[vmem, vmem],
        out_specs=vmem,
        compiler_params=params(8),
        name="pack",
    )(pack, parts)
    moved = exchange(packed, ("ctx", "yb", "zb"), orders[1])

    terms = pl.pallas_call(
        lambda *refs: expert_kernel(ctx_count, orders[1], orders[2], *refs),
        out_shape=jax.ShapeDtypeStruct((ctx_count * dp_count, size, LANES), BF16),
        in_specs=[vmem] * 4,
        out_specs=vmem,
        compiler_params=params(16),
        name="expert",
    )(moved, w_gate[0], w_up[0], down)
    back = exchange(terms, ("ctx",) + DP, orders[2])

    per_owner = pl.pallas_call(
        lambda *refs: combine_kernel(ctx_count, orders[2], orders[3], *refs),
        out_shape=jax.ShapeDtypeStruct((tp_count, CUTS * 2 * tok_rows, LANES), BF16),
        in_specs=[vmem] * 2,
        out_specs=vmem,
        compiler_params=params(8),
        name="combine",
    )(mix, back)
    got = exchange(per_owner, TP, orders[3])

    out = jax.ShapeDtypeStruct((tok_rows, width // dp_count), BF16)
    mixed, input_grad = pl.pallas_call(
        finish_kernel,
        out_shape=(out, out),
        in_specs=[vmem],
        out_specs=(vmem, vmem),
        compiler_params=params(4),
        name="finish",
    )(got)
    return mixed[None], input_grad[None]


def solution(mesh):
    dp_count, ctx_count, tp_count = (mesh.shape[axis] for axis in ("dp", "ctx", "tp"))
    z_count = tp_count // X_PARTS
    fine = Mesh(
        mesh.devices.reshape(dp_count // 2, 2, ctx_count, z_count // 2, 2, X_PARTS),
        ("ya", "yb", "ctx", "za", "zb", "xh"),
    )
    experts = ("ctx",) + TP
    placed = (
        P("ctx", DP, None),
        P("ctx", DP, None),
        P("ctx", None, None),
        P("ctx", None, None),
        P(experts, None, DP),
        P(experts, None, DP),
        P(experts, DP, None),
    )
    return jax.shard_map(
        body,
        mesh=fine,
        in_specs=placed,
        out_specs=(P("ctx", TP, DP), P("ctx", TP, DP)),
        check_vma=False,
    )
```

```python
import jax
import jax.numpy as jnp
from jax import lax
from jax.experimental import pallas as pl
from jax.experimental.pallas import tpu as pltpu
from jax.sharding import Mesh, PartitionSpec as P

BF16 = jnp.bfloat16
F32 = jnp.float32
I32 = jnp.int32
DP = ("ya", "yb")
TP = ("za", "zb", "xh")
X_PARTS = 4
CAP = 6
ROWS = 8
CUTS = 4
LANES = 128


def exchange(v, axes, order):
    return lax.all_to_all(
        v, axes, split_axis=0, concat_axis=0, axis_index_groups=[order], tiled=True
    )


def sixth(v):
    return (v * 10923) >> 16


def iota(shape, dim):
    return lax.broadcasted_iota(I32, shape, dim)


def dot(left, right):
    return jnp.dot(left, right, preferred_element_type=F32)


def dot_t(left, right):
    return lax.dot_general(
        left, right, (((1,), (1,)), ((), ())), preferred_element_type=F32
    )


def in_hbm(v):
    return pltpu.with_memory_space_constraint(v, pltpu.HBM)


def params(mib):
    return pltpu.CompilerParams(vmem_limit_bytes=mib << 20)


def selectors(ctx_count, tp_count, place, routes_ref, probs_ref, pack_ref, mix_ref):
    za, zb, xh = place
    top, column = routes_ref.shape
    columns = 2 * column
    experts = ctx_count * tp_count
    expert = iota((experts, columns), 0).astype(F32)
    named = jnp.zeros((experts, columns), F32)
    share = jnp.zeros((experts, columns), F32)

    def token(j):
        return ((j >> 4) << 3) + (j & 7)

    def kind_of(j):
        return (j >> 3) & 1

    shape = (column, columns)
    spread = (iota(shape, 0) == token(iota(shape, 1))).astype(F32).astype(BF16)
    routes = dot(routes_ref[...].astype(F32).astype(BF16), spread)
    probs = dot(probs_ref[...], spread)
    for k in range(top):
        hit = routes[k : k + 1, :] == expert
        named = jnp.where(hit, 1.0, named)
        share = jnp.where(hit, probs[k : k + 1, :], share)

    row, col = iota((columns, columns), 0), iota((columns, columns), 1)
    earlier = ((kind_of(row) == 0) & (token(row) < token(col))).astype(F32).astype(BF16)
    named = named.astype(BF16)
    before = dot(named, earlier)
    table = jnp.concatenate((named, share.astype(BF16), before.astype(BF16)), axis=1)

    def picked(expert_rows, slot_rows):
        wanted = (expert_rows == iota(expert_rows.shape, 1)).astype(F32).astype(BF16)
        got = dot(wanted, table)
        valid = (got[:, :columns] > 0.5) & (
            got[:, 2 * columns :] == slot_rows.astype(F32)
        )
        return valid, got[:, columns : 2 * columns]

    row = iota((ctx_count * 2 * CUTS * 2 * CAP, LANES), 0)
    outer = sixth(row)
    slot = row - CAP * outer
    kind = outer & 1
    cut = (outer >> 1) & 3
    far = outer >> 3
    owner = (far >> 1) * tp_count + (za * 2 + (far & 1)) * X_PARTS + xh
    valid, scale = picked(owner, slot)
    mine = valid & (kind == kind_of(iota(row.shape, 1)))
    value = jnp.where(mine, jnp.where(kind == 1, scale, 1.0), 0.0)
    for c in range(CUTS):
        pack_ref[:, c * LANES : (c + 1) * LANES] = jnp.where(cut == c, value, 0.0).astype(BF16)

    row = iota((ctx_count * CUTS * 2 * CAP, LANES), 0)
    outer = sixth(row)
    slot = row - CAP * outer
    kind = outer & 1
    owner = (outer >> 3) * tp_count + (za * 2 + zb) * X_PARTS + xh
    valid, scale = picked(owner, slot)
    value = jnp.where(valid, jnp.where(kind == 0, scale, 1.0), 0.0).astype(BF16)
    shape = (mix_ref.shape[0], LANES)
    row, col = iota(shape, 0), iota(shape, 1)
    wanted = (kind_of(col) == 0) & (token(col) == ((row >> 4) << 1) + (row & 1))
    full = dot_t(wanted.astype(F32).astype(BF16), value)
    row, col = iota(full.shape, 0), sixth(iota(full.shape, 1))
    same = (((row >> 1) & 1) == (col & 1)) & (((row >> 2) & 3) == ((col >> 1) & 3))
    mix_ref[...] = jnp.where(same, full, 0.0).astype(BF16)


def first_kernel(
    ctx_count, tp_count, order, tok_ref, cot_ref, routes_ref, probs_ref, weight_ref,
    out_ref, pack_ref, mix_ref, weight_out, held, routes, probs, sems,
):
    za, zb, xh = (lax.axis_index(axis) for axis in TP)
    block = out_ref.shape[3]
    small = [
        pltpu.make_async_copy(ref, to, sems.at[4 + i])
        for i, (ref, to) in enumerate(((routes_ref, routes), (probs_ref, probs)))
    ]
    copies = []
    for yb in range(2):
        for kind, ref in enumerate((tok_ref, cot_ref)):
            start = pl.multiple_of((yb * 2 + zb) * block, block)
            copies.append(
                pltpu.make_async_copy(
                    ref.at[0, :, pl.ds(start, block)], held.at[yb, kind], sems.at[2 * yb + kind]
                )
            )
    weight_copy = pltpu.make_async_copy(weight_ref.at[0], weight_out, sems.at[6])
    for copy in small + copies + [weight_copy]:
        copy.start()
    for copy in small:
        copy.wait()
    selectors(ctx_count, tp_count, (za, zb, xh), routes, probs, pack_ref, mix_ref)
    for yb in range(2):
        for kind in range(2):
            copies[2 * yb + kind].wait()
            value = held[yb, kind]
            for place, d in enumerate(order):
                if d % 2 == yb:
                    out_ref[place, kind] = value
    weight_copy.wait()


def pack_kernel(order_in, order_out, pack_ref, got_ref, out_ref):
    sources, rows, block = got_ref.shape
    got = jnp.concatenate([got_ref[order_in.index(d)] for d in range(sources)], axis=0)
    part = block // CUTS
    stacked = jnp.concatenate([got[:, c * part : (c + 1) * part] for c in range(CUTS)], axis=0)
    packed = dot(pack_ref[...], stacked).astype(BF16)
    size = out_ref.shape[1]
    for place, to in enumerate(order_out):
        c, zb = to >> 2, to & 1
        first = (c * 2 + zb) * size
        out_ref[place] = packed[first : first + size]


def expert_kernel(ctx_count, order_in, order_out, got_ref, gate_ref, up_ref, down_ref, out_ref):
    _, size, part = got_ref.shape
    blocks = got_ref.shape[0] // ctx_count
    width, hidden_rows = gate_ref.shape
    slot_rows = ctx_count * ROWS
    arrived = jnp.concatenate(
        [
            jnp.concatenate([got_ref[order_in.index(c * blocks + q)] for q in range(blocks)], axis=1)
            for c in range(ctx_count)
        ],
        axis=0,
    )

    def source(v):
        slot, c, kind, cut = v & 7, (v >> 3) & 3, (v >> 5) & 1, v >> 6
        return jnp.where(slot < CAP, ((c * CUTS + cut) * 2 + kind) * CAP + slot, -1)

    shape = (CUTS * 2 * slot_rows, ctx_count * size)
    order = (source(iota(shape, 0)) == iota(shape, 1)).astype(F32).astype(BF16)
    sorted_rows = dot(order, arrived).astype(BF16)

    def whole(kind):
        pieces = []
        for q in range(blocks):
            for cut in range(CUTS):
                first = (cut * 2 + kind) * slot_rows
                pieces.append(sorted_rows[first : first + slot_rows, q * part : (q + 1) * part])
        return jnp.concatenate(pieces, axis=1)

    expert_x, expert_dy = whole(0), whole(1)
    into = jnp.concatenate((gate_ref[...], up_ref[...]), axis=1)
    pre = dot(expert_x, into)
    gate_pre, up_pre = pre[:, :hidden_rows], pre[:, hidden_rows:]
    hidden_grad = dot_t(down_ref[...], expert_dy).T
    sigmoid_gate = jax.nn.sigmoid(gate_pre)
    hidden = (gate_pre * sigmoid_gate * up_pre).astype(BF16)
    gate_grad = (
        hidden_grad * up_pre * sigmoid_gate * (1.0 + gate_pre * (1.0 - sigmoid_gate))
    ).astype(BF16)
    up_grad = (hidden_grad * gate_pre * sigmoid_gate).astype(BF16)
    out_term = dot(hidden, down_ref[...]).astype(BF16)
    input_term = dot_t(jnp.concatenate((gate_grad, up_grad), axis=1), into).astype(BF16)

    dp_count = out_ref.shape[0] // ctx_count
    step = width // dp_count
    groups = []
    for cut in range(CUTS):
        for term in (out_term, input_term):
            groups.append(
                jnp.concatenate(
                    [
                        term[:, d * step + cut * LANES : d * step + (cut + 1) * LANES]
                        for d in range(dp_count)
                    ],
                    axis=1,
                )
            )
    shape = (shape[1], shape[0])
    order = (source(iota(shape, 1)) == iota(shape, 0)).astype(F32).astype(BF16)
    leaving = dot(order, jnp.concatenate(groups, axis=0)).astype(BF16)
    for place, to in enumerate(order_out):
        c, d = to // dp_count, to % dp_count
        out_ref[place] = leaving[c * size : (c + 1) * size, d * LANES : (d + 1) * LANES]


def combine_kernel(ctx_count, order_in, order_out, mix_ref, got_ref, out_ref):
    dp_count = got_ref.shape[0] // ctx_count
    sums = []
    for c in range(ctx_count):
        total = got_ref[order_in.index(c * dp_count)].astype(F32)
        for d in range(1, dp_count):
            total = total + got_ref[order_in.index(c * dp_count + d)].astype(F32)
        sums.append(total)
    rows = jnp.concatenate(sums, axis=0).astype(BF16)
    mixed = dot(mix_ref[...], rows).astype(BF16).reshape(out_ref.shape)
    for place, to in enumerate(order_out):
        out_ref[place] = mixed[to]


def finish_kernel(got_ref, mixed_ref, grad_ref):
    total = jnp.sum(got_ref[...].astype(F32), axis=0)
    count = mixed_ref.shape[0]
    for cut in range(CUTS):
        lanes = slice(cut * LANES, (cut + 1) * LANES)
        first = cut * 2 * count
        mixed_ref[:, lanes] = total[first : first + count].astype(BF16)
        grad_ref[:, lanes] = total[first + count : first + 2 * count].astype(BF16)


def body(tokens, cotangent, routes, probs, w_gate, w_up, w_down):
    dp_count = lax.axis_size("ya") * lax.axis_size("yb")
    ctx_count = lax.axis_size("ctx")
    tp_count = lax.axis_size("za") * lax.axis_size("zb") * lax.axis_size("xh")
    _, own_rows, width = tokens.shape
    column, top = routes.shape[1:]
    dp_order = [(4 + step) % dp_count for step in (0, 4, 1, 5, 7, 3, 6, 2)]
    orders = (
        dp_order,
        [(1 + 7 * j) % (ctx_count * 4) for j in range(ctx_count * 4)],
        [
            (j // dp_count + 3 * j) % ctx_count * dp_count + (4 + 5 * j) % dp_count
            for j in range(ctx_count * dp_count)
        ],
        [
            (7 + 5 * j) % (tp_count // X_PARTS) * X_PARTS
            + (2 + j // (tp_count // X_PARTS) + 3 * j) % X_PARTS
            for j in range(tp_count)
        ],
    )
    block = width // 4
    size = CUTS * 2 * CAP
    tok_rows = column // tp_count
    any_space = pl.BlockSpec(memory_space=pl.ANY)
    vmem = pl.BlockSpec(memory_space=pltpu.VMEM)

    spread, pack, mix, down = pl.pallas_call(
        lambda *refs: first_kernel(ctx_count, tp_count, orders[0], *refs),
        out_shape=(
            pltpu.VMEM((dp_count, 2, own_rows, block), BF16),
            pltpu.VMEM((ctx_count * 2 * size, CUTS * 2 * column), BF16),
            pltpu.VMEM((tp_count * CUTS * 2 * tok_rows, ctx_count * size), BF16),
            pltpu.VMEM(w_down.shape[1:], BF16),
        ),
        in_specs=[any_space] * 5,
        out_specs=(vmem,) * 4,
        scratch_shapes=[
            pltpu.VMEM((2, 2, own_rows, block), BF16),
            pltpu.VMEM((top, column), I32),
            pltpu.VMEM((top, column), BF16),
            pltpu.SemaphoreType.DMA((7,)),
        ],
        compiler_params=params(8),
        name="first",
    )(*(in_hbm(v) for v in (tokens, cotangent, routes[0].T, probs[0].T, w_down)))
    parts = exchange(spread, DP, orders[0])
    parts = parts.reshape(dp_count, 2 * own_rows, block)

    packed = pl.pallas_call(
        lambda *refs: pack_kernel(orders[0], orders[1], *refs),
        out_shape=jax.ShapeDtypeStruct((ctx_count * 4, size, block // CUTS), BF16),
        in_specs=[vmem, vmem],
        out_specs=vmem,
        compiler_params=params(8),
        name="pack",
    )(pack, parts)
    moved = exchange(packed, ("ctx", "yb", "zb"), orders[1])

    terms = pl.pallas_call(
        lambda *refs: expert_kernel(ctx_count, orders[1], orders[2], *refs),
        out_shape=jax.ShapeDtypeStruct((ctx_count * dp_count, size, LANES), BF16),
        in_specs=[vmem] * 4,
        out_specs=vmem,
        compiler_params=params(16),
        name="expert",
    )(moved, w_gate[0], w_up[0], down)
    back = exchange(terms, ("ctx",) + DP, orders[2])

    per_owner = pl.pallas_call(
        lambda *refs: combine_kernel(ctx_count, orders[2], orders[3], *refs),
        out_shape=jax.ShapeDtypeStruct((tp_count, CUTS * 2 * tok_rows, LANES), BF16),
        in_specs=[vmem] * 2,
        out_specs=vmem,
        compiler_params=params(8),
        name="combine",
    )(mix, back)
    got = exchange(per_owner, TP, orders[3])

    out = jax.ShapeDtypeStruct((tok_rows, width // dp_count), BF16)
    mixed, input_grad = pl.pallas_call(
        finish_kernel,
        out_shape=(out, out),
        in_specs=[vmem],
        out_specs=(vmem, vmem),
        compiler_params=params(4),
        name="finish",
    )(got)
    return mixed[None], input_grad[None]


def solution(mesh):
    dp_count, ctx_count, tp_count = (mesh.shape[axis] for axis in ("dp", "ctx", "tp"))
    z_count = tp_count // X_PARTS
    fine = Mesh(
        mesh.devices.reshape(dp_count // 2, 2, ctx_count, z_count // 2, 2, X_PARTS),
        ("ya", "yb", "ctx", "za", "zb", "xh"),
    )
    experts = ("ctx",) + TP
    placed = (
        P("ctx", DP, None),
        P("ctx", DP, None),
        P("ctx", None, None),
        P("ctx", None, None),
        P(experts, None, DP),
        P(experts, None, DP),
        P(experts, DP, None),
    )
    return jax.shard_map(
        body,
        mesh=fine,
        in_specs=placed,
        out_specs=(P("ctx", TP, DP), P("ctx", TP, DP)),
        check_vma=False,
    )
```

```python
import jax
import jax.numpy as jnp
from jax import lax
from jax.experimental import pallas as pl
from jax.experimental.pallas import tpu as pltpu
from jax.sharding import Mesh, PartitionSpec as P

BF16 = jnp.bfloat16
F32 = jnp.float32
I32 = jnp.int32
DP = ("ya", "yb")
TP = ("za", "zb", "xh")
X_PARTS = 4
CAP = 6
ROWS = 8
CUTS = 4
LANES = 128


def exchange(v, axes, order):
    return lax.all_to_all(
        v, axes, split_axis=0, concat_axis=0, axis_index_groups=[order], tiled=True
    )


def sixth(v):
    return (v * 10923) >> 16


def iota(shape, dim):
    return lax.broadcasted_iota(I32, shape, dim)


def dot(left, right):
    return jnp.dot(left, right, preferred_element_type=F32)


def dot_t(left, right):
    return lax.dot_general(
        left, right, (((1,), (1,)), ((), ())), preferred_element_type=F32
    )


def in_hbm(v):
    return pltpu.with_memory_space_constraint(v, pltpu.HBM)


def params(mib):
    return pltpu.CompilerParams(vmem_limit_bytes=mib << 20)


def selectors(ctx_count, tp_count, place, routes_ref, probs_ref, pack_ref, mix_ref):
    za, zb, xh = place
    top, column = routes_ref.shape
    columns = 2 * column
    experts = ctx_count * tp_count
    expert = iota((experts, columns), 0).astype(F32)
    named = jnp.zeros((experts, columns), F32)
    share = jnp.zeros((experts, columns), F32)

    def token(j):
        return ((j >> 4) << 3) + (j & 7)

    def kind_of(j):
        return (j >> 3) & 1

    shape = (column, columns)
    spread = (iota(shape, 0) == token(iota(shape, 1))).astype(F32).astype(BF16)
    routes = dot(routes_ref[...].astype(F32).astype(BF16), spread)
    probs = dot(probs_ref[...], spread)
    for k in range(top):
        hit = routes[k : k + 1, :] == expert
        named = jnp.where(hit, 1.0, named)
        share = jnp.where(hit, probs[k : k + 1, :], share)

    row, col = iota((columns, columns), 0), iota((columns, columns), 1)
    earlier = ((kind_of(row) == 0) & (token(row) < token(col))).astype(F32).astype(BF16)
    named = named.astype(BF16)
    before = dot(named, earlier)
    table = jnp.concatenate((named, share.astype(BF16), before.astype(BF16)), axis=1)

    def picked(expert_rows, slot_rows):
        wanted = (expert_rows == iota(expert_rows.shape, 1)).astype(F32).astype(BF16)
        got = dot(wanted, table)
        valid = (got[:, :columns] > 0.5) & (
            got[:, 2 * columns :] == slot_rows.astype(F32)
        )
        return valid, got[:, columns : 2 * columns]

    row = iota((ctx_count * 2 * CUTS * 2 * CAP, LANES), 0)
    outer = sixth(row)
    slot = row - CAP * outer
    kind = outer & 1
    cut = (outer >> 1) & 3
    far = outer >> 3
    owner = (far >> 1) * tp_count + (za * 2 + (far & 1)) * X_PARTS + xh
    valid, scale = picked(owner, slot)
    mine = valid & (kind == kind_of(iota(row.shape, 1)))
    value = jnp.where(mine, jnp.where(kind == 1, scale, 1.0), 0.0)
    for c in range(CUTS):
        pack_ref[:, c * LANES : (c + 1) * LANES] = jnp.where(cut == c, value, 0.0).astype(BF16)

    row = iota((ctx_count * CUTS * 2 * CAP, LANES), 0)
    outer = sixth(row)
    slot = row - CAP * outer
    kind = outer & 1
    owner = (outer >> 3) * tp_count + (za * 2 + zb) * X_PARTS + xh
    valid, scale = picked(owner, slot)
    value = jnp.where(valid, jnp.where(kind == 0, scale, 1.0), 0.0).astype(BF16)
    shape = (mix_ref.shape[0], LANES)
    row, col = iota(shape, 0), iota(shape, 1)
    wanted = (kind_of(col) == 0) & (token(col) == ((row >> 4) << 1) + (row & 1))
    full = dot_t(wanted.astype(F32).astype(BF16), value)
    row, col = iota(full.shape, 0), sixth(iota(full.shape, 1))
    same = (((row >> 1) & 1) == (col & 1)) & (((row >> 2) & 3) == ((col >> 1) & 3))
    mix_ref[...] = jnp.where(same, full, 0.0).astype(BF16)


def first_kernel(
    ctx_count, tp_count, order, tok_ref, cot_ref, routes_ref, probs_ref, weight_ref,
    out_ref, pack_ref, mix_ref, weight_out, held, routes, probs, sems,
):
    za, zb, xh = (lax.axis_index(axis) for axis in TP)
    block = out_ref.shape[3]
    small = [
        pltpu.make_async_copy(ref, to, sems.at[4 + i])
        for i, (ref, to) in enumerate(((routes_ref, routes), (probs_ref, probs)))
    ]
    copies = []
    for yb in range(2):
        for kind, ref in enumerate((tok_ref, cot_ref)):
            start = pl.multiple_of((yb * 2 + zb) * block, block)
            copies.append(
                pltpu.make_async_copy(
                    ref.at[0, :, pl.ds(start, block)], held.at[yb, kind], sems.at[2 * yb + kind]
                )
            )
    weight_copy = pltpu.make_async_copy(weight_ref.at[0], weight_out, sems.at[6])
    for copy in small + copies + [weight_copy]:
        copy.start()
    for copy in small:
        copy.wait()
    selectors(ctx_count, tp_count, (za, zb, xh), routes, probs, pack_ref, mix_ref)
    for yb in range(2):
        for kind in range(2):
            copies[2 * yb + kind].wait()
            value = held[yb, kind]
            for place, d in enumerate(order):
                if d % 2 == yb:
                    out_ref[place, kind] = value
    weight_copy.wait()


def pack_kernel(order_in, order_out, pack_ref, got_ref, out_ref):
    sources, rows, block = got_ref.shape
    got = jnp.concatenate([got_ref[order_in.index(d)] for d in range(sources)], axis=0)
    part = block // CUTS
    stacked = jnp.concatenate([got[:, c * part : (c + 1) * part] for c in range(CUTS)], axis=0)
    packed = dot(pack_ref[...], stacked).astype(BF16)
    size = out_ref.shape[1]
    for place, to in enumerate(order_out):
        c, zb = to >> 2, to & 1
        first = (c * 2 + zb) * size
        out_ref[place] = packed[first : first + size]


def expert_kernel(ctx_count, order_in, order_out, got_ref, gate_ref, up_ref, down_ref, out_ref):
    _, size, part = got_ref.shape
    blocks = got_ref.shape[0] // ctx_count
    width, hidden_rows = gate_ref.shape
    slot_rows = ctx_count * ROWS
    arrived = jnp.concatenate(
        [
            jnp.concatenate([got_ref[order_in.index(c * blocks + q)] for q in range(blocks)], axis=1)
            for c in range(ctx_count)
        ],
        axis=0,
    )

    def source(v):
        slot, c, kind, cut = v & 7, (v >> 3) & 3, (v >> 5) & 1, v >> 6
        return jnp.where(slot < CAP, ((c * CUTS + cut) * 2 + kind) * CAP + slot, -1)

    shape = (CUTS * 2 * slot_rows, ctx_count * size)
    order = (source(iota(shape, 0)) == iota(shape, 1)).astype(F32).astype(BF16)
    sorted_rows = dot(order, arrived).astype(BF16)

    def whole(kind):
        pieces = []
        for q in range(blocks):
            for cut in range(CUTS):
                first = (cut * 2 + kind) * slot_rows
                pieces.append(sorted_rows[first : first + slot_rows, q * part : (q + 1) * part])
        return jnp.concatenate(pieces, axis=1)

    expert_x, expert_dy = whole(0), whole(1)
    into = jnp.concatenate((gate_ref[...], up_ref[...]), axis=1)
    pre = dot(expert_x, into)
    gate_pre, up_pre = pre[:, :hidden_rows], pre[:, hidden_rows:]
    hidden_grad = dot_t(down_ref[...], expert_dy).T
    sigmoid_gate = jax.nn.sigmoid(gate_pre)
    hidden = (gate_pre * sigmoid_gate * up_pre).astype(BF16)
    gate_grad = (
        hidden_grad * up_pre * sigmoid_gate * (1.0 + gate_pre * (1.0 - sigmoid_gate))
    ).astype(BF16)
    up_grad = (hidden_grad * gate_pre * sigmoid_gate).astype(BF16)
    out_term = dot(hidden, down_ref[...]).astype(BF16)
    input_term = dot_t(jnp.concatenate((gate_grad, up_grad), axis=1), into).astype(BF16)

    dp_count = out_ref.shape[0] // ctx_count
    step = width // dp_count
    groups = []
    for cut in range(CUTS):
        for term in (out_term, input_term):
            groups.append(
                jnp.concatenate(
                    [
                        term[:, d * step + cut * LANES : d * step + (cut + 1) * LANES]
                        for d in range(dp_count)
                    ],
                    axis=1,
                )
            )
    shape = (shape[1], shape[0])
    order = (source(iota(shape, 1)) == iota(shape, 0)).astype(F32).astype(BF16)
    leaving = dot(order, jnp.concatenate(groups, axis=0)).astype(BF16)
    for place, to in enumerate(order_out):
        c, d = to // dp_count, to % dp_count
        out_ref[place] = leaving[c * size : (c + 1) * size, d * LANES : (d + 1) * LANES]


def combine_kernel(ctx_count, order_in, order_out, mix_ref, got_ref, out_ref):
    dp_count = got_ref.shape[0] // ctx_count
    sums = []
    for c in range(ctx_count):
        total = got_ref[order_in.index(c * dp_count)].astype(F32)
        for d in range(1, dp_count):
            total = total + got_ref[order_in.index(c * dp_count + d)].astype(F32)
        sums.append(total)
    rows = jnp.concatenate(sums, axis=0).astype(BF16)
    mixed = dot(mix_ref[...], rows).astype(BF16).reshape(out_ref.shape)
    for place, to in enumerate(order_out):
        out_ref[place] = mixed[to]


def finish_kernel(got_ref, mixed_ref, grad_ref):
    total = jnp.sum(got_ref[...].astype(F32), axis=0)
    count = mixed_ref.shape[0]
    for cut in range(CUTS):
        lanes = slice(cut * LANES, (cut + 1) * LANES)
        first = cut * 2 * count
        mixed_ref[:, lanes] = total[first : first + count].astype(BF16)
        grad_ref[:, lanes] = total[first + count : first + 2 * count].astype(BF16)


def body(tokens, cotangent, routes, probs, w_gate, w_up, w_down):
    dp_count = lax.axis_size("ya") * lax.axis_size("yb")
    ctx_count = lax.axis_size("ctx")
    tp_count = lax.axis_size("za") * lax.axis_size("zb") * lax.axis_size("xh")
    _, own_rows, width = tokens.shape
    column, top = routes.shape[1:]
    orders = (
        [(4 + 3 * j) % dp_count for j in range(dp_count)],
        [(1 + 7 * j) % (ctx_count * 4) for j in range(ctx_count * 4)],
        [
            (j // dp_count + 3 * j) % ctx_count * dp_count + (4 + 5 * j) % dp_count
            for j in range(ctx_count * dp_count)
        ],
        [
            (7 + 5 * j) % (tp_count // X_PARTS) * X_PARTS
            + (2 + j // (tp_count // X_PARTS) + 3 * j) % X_PARTS
            for j in range(tp_count)
        ],
    )
    block = width // 4
    size = CUTS * 2 * CAP
    tok_rows = column // tp_count
    any_space = pl.BlockSpec(memory_space=pl.ANY)
    vmem = pl.BlockSpec(memory_space=pltpu.VMEM)

    spread, pack, mix, down = pl.pallas_call(
        lambda *refs: first_kernel(ctx_count, tp_count, orders[0], *refs),
        out_shape=(
            pltpu.VMEM((dp_count, 2, own_rows, block), BF16),
            pltpu.VMEM((ctx_count * 2 * size, CUTS * 2 * column), BF16),
            pltpu.VMEM((tp_count * CUTS * 2 * tok_rows, ctx_count * size), BF16),
            pltpu.VMEM(w_down.shape[1:], BF16),
        ),
        in_specs=[any_space] * 5,
        out_specs=(vmem,) * 4,
        scratch_shapes=[
            pltpu.VMEM((2, 2, own_rows, block), BF16),
            pltpu.VMEM((top, column), I32),
            pltpu.VMEM((top, column), BF16),
            pltpu.SemaphoreType.DMA((7,)),
        ],
        compiler_params=params(8),
        name="first",
    )(*(in_hbm(v) for v in (tokens, cotangent, routes[0].T, probs[0].T, w_down)))
    parts = exchange(spread, DP, orders[0])
    parts = parts.reshape(dp_count, 2 * own_rows, block)

    packed = pl.pallas_call(
        lambda *refs: pack_kernel(orders[0], orders[1], *refs),
        out_shape=jax.ShapeDtypeStruct((ctx_count * 4, size, block // CUTS), BF16),
        in_specs=[vmem, vmem],
        out_specs=vmem,
        compiler_params=params(8),
        name="pack",
    )(pack, parts)
    moved = exchange(packed, ("ctx", "yb", "zb"), orders[1])

    terms = pl.pallas_call(
        lambda *refs: expert_kernel(ctx_count, orders[1], orders[2], *refs),
        out_shape=jax.ShapeDtypeStruct((ctx_count * dp_count, size, LANES), BF16),
        in_specs=[vmem] * 4,
        out_specs=vmem,
        compiler_params=params(16),
        name="expert",
    )(moved, w_gate[0], w_up[0], down)
    back = exchange(terms, ("ctx",) + DP, orders[2])

    per_owner = pl.pallas_call(
        lambda *refs: combine_kernel(ctx_count, orders[2], orders[3], *refs),
        out_shape=jax.ShapeDtypeStruct((tp_count, CUTS * 2 * tok_rows, LANES), BF16),
        in_specs=[vmem] * 2,
        out_specs=vmem,
        compiler_params=params(8),
        name="combine",
    )(mix, back)
    got = exchange(per_owner, TP, orders[3])

    out = jax.ShapeDtypeStruct((tok_rows, width // dp_count), BF16)
    mixed, input_grad = pl.pallas_call(
        finish_kernel,
        out_shape=(out, out),
        in_specs=[vmem],
        out_specs=(vmem, vmem),
        compiler_params=params(4),
        name="finish",
    )(got)
    return mixed[None], input_grad[None]


def solution(mesh):
    dp_count, ctx_count, tp_count = (mesh.shape[axis] for axis in ("dp", "ctx", "tp"))
    z_count = tp_count // X_PARTS
    fine = Mesh(
        mesh.devices.reshape(dp_count // 2, 2, ctx_count, z_count // 2, 2, X_PARTS),
        ("ya", "yb", "ctx", "za", "zb", "xh"),
    )
    experts = ("ctx",) + TP
    placed = (
        P("ctx", DP, None),
        P("ctx", DP, None),
        P("ctx", None, None),
        P("ctx", None, None),
        P(experts, None, DP),
        P(experts, None, DP),
        P(experts, DP, None),
    )
    return jax.shard_map(
        body,
        mesh=fine,
        in_specs=placed,
        out_specs=(P("ctx", TP, DP), P("ctx", TP, DP)),
        check_vma=False,
    )
```

```python
import jax
import jax.numpy as jnp
from jax import lax
from jax.experimental import pallas as pl
from jax.experimental.pallas import tpu as pltpu
from jax.sharding import Mesh, PartitionSpec as P

BF16 = jnp.bfloat16
F32 = jnp.float32
I32 = jnp.int32
DP = ("ya", "yb")
TP = ("za", "zb", "xh")
X_PARTS = 4
CAP = 6
ROWS = 8
CUTS = 4
LANES = 128


def exchange(v, axes, order):
    return lax.all_to_all(
        v, axes, split_axis=0, concat_axis=0, axis_index_groups=[order], tiled=True
    )


def sixth(v):
    return (v * 10923) >> 16


def iota(shape, dim):
    return lax.broadcasted_iota(I32, shape, dim)


def dot(left, right):
    return jnp.dot(left, right, preferred_element_type=F32)


def dot_t(left, right):
    return lax.dot_general(
        left, right, (((1,), (1,)), ((), ())), preferred_element_type=F32
    )


def in_hbm(v):
    return pltpu.with_memory_space_constraint(v, pltpu.HBM)


def params(mib):
    return pltpu.CompilerParams(vmem_limit_bytes=mib << 20)


def selectors(ctx_count, tp_count, place, routes_ref, probs_ref, pack_ref, mix_ref):
    za, zb, xh = place
    top, column = routes_ref.shape
    columns = 2 * column
    experts = ctx_count * tp_count
    expert = iota((experts, columns), 0).astype(F32)
    named = jnp.zeros((experts, columns), F32)
    share = jnp.zeros((experts, columns), F32)

    def token(j):
        return ((j >> 4) << 3) + (j & 7)

    def kind_of(j):
        return (j >> 3) & 1

    shape = (column, columns)
    spread = (iota(shape, 0) == token(iota(shape, 1))).astype(F32).astype(BF16)
    both = jnp.concatenate((routes_ref[...].astype(F32), probs_ref[...].astype(F32)), axis=0)
    both = dot(both.astype(BF16), spread)
    routes, probs = both[:top], both[top:]
    for k in range(top):
        hit = routes[k : k + 1, :] == expert
        named = jnp.where(hit, 1.0, named)
        share = jnp.where(hit, probs[k : k + 1, :], share)

    row, col = iota((columns, columns), 0), iota((columns, columns), 1)
    earlier = ((kind_of(row) == 0) & (token(row) < token(col))).astype(F32).astype(BF16)
    named = named.astype(BF16)
    before = dot(named, earlier)
    table = jnp.concatenate((named, share.astype(BF16), before.astype(BF16)), axis=1)

    def parts(rows):
        row = iota((rows, LANES), 0)
        outer = sixth(row)
        return row - CAP * outer, outer & 1, (outer >> 1) & 3, outer >> 3

    slot, kind, cut, far = parts(ctx_count * 2 * CUTS * 2 * CAP)
    owner = (far >> 1) * tp_count + (za * 2 + (far & 1)) * X_PARTS + xh
    own_slot, own_kind, _, own_far = parts(ctx_count * CUTS * 2 * CAP)
    own_owner = own_far * tp_count + (za * 2 + zb) * X_PARTS + xh
    owners = jnp.concatenate((owner, own_owner), axis=0)
    slots = jnp.concatenate((slot, own_slot), axis=0).astype(F32)
    got = dot((owners == iota(owners.shape, 1)).astype(F32).astype(BF16), table)
    valid = (got[:, :columns] > 0.5) & (got[:, 2 * columns :] == slots)
    scale = got[:, columns : 2 * columns]
    count = slot.shape[0]

    mine = valid[:count] & (kind == kind_of(iota(slot.shape, 1)))
    value = jnp.where(mine, jnp.where(kind == 1, scale[:count], 1.0), 0.0)
    for c in range(CUTS):
        pack_ref[:, c * LANES : (c + 1) * LANES] = jnp.where(cut == c, value, 0.0).astype(BF16)

    value = jnp.where(
        valid[count:], jnp.where(own_kind == 0, scale[count:], 1.0), 0.0
    ).astype(BF16)
    shape = (mix_ref.shape[0], LANES)
    row, col = iota(shape, 0), iota(shape, 1)
    wanted = (kind_of(col) == 0) & (token(col) == ((row >> 4) << 1) + (row & 1))
    full = dot_t(wanted.astype(F32).astype(BF16), value)
    row, col = iota(full.shape, 0), sixth(iota(full.shape, 1))
    same = (((row >> 1) & 1) == (col & 1)) & (((row >> 2) & 3) == ((col >> 1) & 3))
    mix_ref[...] = jnp.where(same, full, 0.0).astype(BF16)


def first_kernel(
    ctx_count, tp_count, order, tok_ref, cot_ref, routes_ref, probs_ref, weight_ref,
    out_ref, pack_ref, mix_ref, weight_out, held, routes, probs, sems,
):
    za, zb, xh = (lax.axis_index(axis) for axis in TP)
    block = out_ref.shape[3]
    small = [
        pltpu.make_async_copy(ref, to, sems.at[4 + i])
        for i, (ref, to) in enumerate(((routes_ref, routes), (probs_ref, probs)))
    ]
    copies = []
    for yb in range(2):
        for kind, ref in enumerate((tok_ref, cot_ref)):
            start = pl.multiple_of((yb * 2 + zb) * block, block)
            copies.append(
                pltpu.make_async_copy(
                    ref.at[0, :, pl.ds(start, block)], held.at[yb, kind], sems.at[2 * yb + kind]
                )
            )
    weight_copy = pltpu.make_async_copy(weight_ref.at[0], weight_out, sems.at[6])
    for copy in small + copies + [weight_copy]:
        copy.start()
    for copy in small:
        copy.wait()
    selectors(ctx_count, tp_count, (za, zb, xh), routes, probs, pack_ref, mix_ref)
    for yb in range(2):
        for kind in range(2):
            copies[2 * yb + kind].wait()
            value = held[yb, kind]
            for place, d in enumerate(order):
                if d % 2 == yb:
                    out_ref[place, kind] = value
    weight_copy.wait()


def pack_kernel(order_in, order_out, pack_ref, got_ref, out_ref):
    sources, rows, block = got_ref.shape
    got = jnp.concatenate([got_ref[order_in.index(d)] for d in range(sources)], axis=0)
    part = block // CUTS
    stacked = jnp.concatenate([got[:, c * part : (c + 1) * part] for c in range(CUTS)], axis=0)
    packed = dot(pack_ref[...], stacked).astype(BF16)
    size = out_ref.shape[1]
    for place, to in enumerate(order_out):
        c, zb = to >> 2, to & 1
        first = (c * 2 + zb) * size
        out_ref[place] = packed[first : first + size]


def expert_kernel(ctx_count, order_in, order_out, got_ref, gate_ref, up_ref, down_ref, out_ref):
    _, size, part = got_ref.shape
    blocks = got_ref.shape[0] // ctx_count
    width, hidden_rows = gate_ref.shape
    slot_rows = ctx_count * ROWS
    arrived = jnp.concatenate(
        [
            jnp.concatenate([got_ref[order_in.index(c * blocks + q)] for q in range(blocks)], axis=1)
            for c in range(ctx_count)
        ],
        axis=0,
    )

    def source(v):
        slot, c, kind, cut = v & 7, (v >> 3) & 3, (v >> 5) & 1, v >> 6
        return jnp.where(slot < CAP, ((c * CUTS + cut) * 2 + kind) * CAP + slot, -1)

    shape = (CUTS * 2 * slot_rows, ctx_count * size)
    order = (source(iota(shape, 0)) == iota(shape, 1)).astype(F32).astype(BF16)
    sorted_rows = dot(order, arrived).astype(BF16)

    def whole(kind):
        pieces = []
        for q in range(blocks):
            for cut in range(CUTS):
                first = (cut * 2 + kind) * slot_rows
                pieces.append(sorted_rows[first : first + slot_rows, q * part : (q + 1) * part])
        return jnp.concatenate(pieces, axis=1)

    expert_x, expert_dy = whole(0), whole(1)
    into = jnp.concatenate((gate_ref[...], up_ref[...]), axis=1)
    pre = dot(expert_x, into)
    gate_pre, up_pre = pre[:, :hidden_rows], pre[:, hidden_rows:]
    hidden_grad = dot_t(down_ref[...], expert_dy).T
    sigmoid_gate = jax.nn.sigmoid(gate_pre)
    hidden = (gate_pre * sigmoid_gate * up_pre).astype(BF16)
    gate_grad = (
        hidden_grad * up_pre * sigmoid_gate * (1.0 + gate_pre * (1.0 - sigmoid_gate))
    ).astype(BF16)
    up_grad = (hidden_grad * gate_pre * sigmoid_gate).astype(BF16)
    out_term = dot(hidden, down_ref[...]).astype(BF16)
    input_term = dot_t(jnp.concatenate((gate_grad, up_grad), axis=1), into).astype(BF16)

    dp_count = out_ref.shape[0] // ctx_count
    step = width // dp_count
    groups = []
    for cut in range(CUTS):
        for term in (out_term, input_term):
            groups.append(
                jnp.concatenate(
                    [
                        term[:, d * step + cut * LANES : d * step + (cut + 1) * LANES]
                        for d in range(dp_count)
                    ],
                    axis=1,
                )
            )
    shape = (shape[1], shape[0])
    order = (source(iota(shape, 1)) == iota(shape, 0)).astype(F32).astype(BF16)
    leaving = dot(order, jnp.concatenate(groups, axis=0)).astype(BF16)
    for place, to in enumerate(order_out):
        c, d = to // dp_count, to % dp_count
        out_ref[place] = leaving[c * size : (c + 1) * size, d * LANES : (d + 1) * LANES]


def combine_kernel(ctx_count, order_in, order_out, mix_ref, got_ref, out_ref):
    dp_count = got_ref.shape[0] // ctx_count
    sums = []
    for c in range(ctx_count):
        total = got_ref[order_in.index(c * dp_count)].astype(F32)
        for d in range(1, dp_count):
            total = total + got_ref[order_in.index(c * dp_count + d)].astype(F32)
        sums.append(total)
    rows = jnp.concatenate(sums, axis=0).astype(BF16)
    mixed = dot(mix_ref[...], rows).astype(BF16).reshape(out_ref.shape)
    for place, to in enumerate(order_out):
        out_ref[place] = mixed[to]


def finish_kernel(got_ref, mixed_ref, grad_ref):
    total = jnp.sum(got_ref[...].astype(F32), axis=0)
    count = mixed_ref.shape[0]
    for cut in range(CUTS):
        lanes = slice(cut * LANES, (cut + 1) * LANES)
        first = cut * 2 * count
        mixed_ref[:, lanes] = total[first : first + count].astype(BF16)
        grad_ref[:, lanes] = total[first + count : first + 2 * count].astype(BF16)


def body(tokens, cotangent, routes, probs, w_gate, w_up, w_down):
    dp_count = lax.axis_size("ya") * lax.axis_size("yb")
    ctx_count = lax.axis_size("ctx")
    tp_count = lax.axis_size("za") * lax.axis_size("zb") * lax.axis_size("xh")
    _, own_rows, width = tokens.shape
    column, top = routes.shape[1:]
    orders = (
        [(5 + 3 * j) % dp_count for j in range(dp_count)],
        [(1 + 7 * j) % (ctx_count * 4) for j in range(ctx_count * 4)],
        [
            (j // dp_count + 3 * j) % ctx_count * dp_count + (4 + 5 * j) % dp_count
            for j in range(ctx_count * dp_count)
        ],
        [
            (7 + 5 * j) % (tp_count // X_PARTS) * X_PARTS
            + (2 + j // (tp_count // X_PARTS) + 3 * j) % X_PARTS
            for j in range(tp_count)
        ],
    )
    block = width // 4
    size = CUTS * 2 * CAP
    tok_rows = column // tp_count
    any_space = pl.BlockSpec(memory_space=pl.ANY)
    vmem = pl.BlockSpec(memory_space=pltpu.VMEM)

    spread, pack, mix, down = pl.pallas_call(
        lambda *refs: first_kernel(ctx_count, tp_count, orders[0], *refs),
        out_shape=(
            pltpu.VMEM((dp_count, 2, own_rows, block), BF16),
            pltpu.VMEM((ctx_count * 2 * size, CUTS * 2 * column), BF16),
            pltpu.VMEM((tp_count * CUTS * 2 * tok_rows, ctx_count * size), BF16),
            pltpu.VMEM(w_down.shape[1:], BF16),
        ),
        in_specs=[any_space] * 5,
        out_specs=(vmem,) * 4,
        scratch_shapes=[
            pltpu.VMEM((2, 2, own_rows, block), BF16),
            pltpu.VMEM((top, column), I32),
            pltpu.VMEM((top, column), BF16),
            pltpu.SemaphoreType.DMA((7,)),
        ],
        compiler_params=params(8),
        name="first",
    )(*(in_hbm(v) for v in (tokens, cotangent, routes[0].T, probs[0].T, w_down)))
    parts = exchange(spread, DP, orders[0])
    parts = parts.reshape(dp_count, 2 * own_rows, block)

    packed = pl.pallas_call(
        lambda *refs: pack_kernel(orders[0], orders[1], *refs),
        out_shape=jax.ShapeDtypeStruct((ctx_count * 4, size, block // CUTS), BF16),
        in_specs=[vmem, vmem],
        out_specs=vmem,
        compiler_params=params(8),
        name="pack",
    )(pack, parts)
    moved = exchange(packed, ("ctx", "yb", "zb"), orders[1])

    terms = pl.pallas_call(
        lambda *refs: expert_kernel(ctx_count, orders[1], orders[2], *refs),
        out_shape=jax.ShapeDtypeStruct((ctx_count * dp_count, size, LANES), BF16),
        in_specs=[vmem] * 4,
        out_specs=vmem,
        compiler_params=params(16),
        name="expert",
    )(moved, w_gate[0], w_up[0], down)
    back = exchange(terms, ("ctx",) + DP, orders[2])

    per_owner = pl.pallas_call(
        lambda *refs: combine_kernel(ctx_count, orders[2], orders[3], *refs),
        out_shape=jax.ShapeDtypeStruct((tp_count, CUTS * 2 * tok_rows, LANES), BF16),
        in_specs=[vmem] * 2,
        out_specs=vmem,
        compiler_params=params(8),
        name="combine",
    )(mix, back)
    got = exchange(per_owner, TP, orders[3])

    out = jax.ShapeDtypeStruct((tok_rows, width // dp_count), BF16)
    mixed, input_grad = pl.pallas_call(
        finish_kernel,
        out_shape=(out, out),
        in_specs=[vmem],
        out_specs=(vmem, vmem),
        compiler_params=params(4),
        name="finish",
    )(got)
    return mixed[None], input_grad[None]


def solution(mesh):
    dp_count, ctx_count, tp_count = (mesh.shape[axis] for axis in ("dp", "ctx", "tp"))
    z_count = tp_count // X_PARTS
    fine = Mesh(
        mesh.devices.reshape(dp_count // 2, 2, ctx_count, z_count // 2, 2, X_PARTS),
        ("ya", "yb", "ctx", "za", "zb", "xh"),
    )
    experts = ("ctx",) + TP
    placed = (
        P("ctx", DP, None),
        P("ctx", DP, None),
        P("ctx", None, None),
        P("ctx", None, None),
        P(experts, None, DP),
        P(experts, None, DP),
        P(experts, DP, None),
    )
    return jax.shard_map(
        body,
        mesh=fine,
        in_specs=placed,
        out_specs=(P("ctx", TP, DP), P("ctx", TP, DP)),
        check_vma=False,
    )
```
